32 devices in a mesh: elem: 16 (over z, x, core), state: 2 (over y).
Axes of the slice: x: 2, y: 2, z: 4, core: 2. Of those that a mesh axis runs over, the one named last changes fastest.
Arguments:
- orbitals: bfloat16 [192, 160, 256], P(('elem', 'state')), may hold values from -6 to 6
- rotation: bfloat16 [256, 256], replicated, may hold values from -0.375 to 0.375
- counts: int32 [192], P('elem'), may hold values from 96 to 160, as said below
- neighbors: int32 [192, 5], P('elem'), may hold values from 0 to 191, as said below
- blocks: bfloat16 [192, 5, 160, 160], P('elem'), may hold values from -0.21875 to 0.21875
Outputs:
- filtered: bfloat16 [192, 160, 256], P(('elem', 'state'))
The draws below stay inside these ranges and needn't reach their ends.
Inputs may be any that keep to these rules, and one draw needn't show every extreme that they name: `neighbors`: entry 0 of row e is e; every other entry is (e + d) mod 192 with 1 <= |d| <= 4. The adaptive basis is sized per pair of neighbouring elements: over each aligned block of 6 elements the counts sum to at most 864, and the first block of every index of elem sums to exactly 864.
All inputs are finite; a program needn't handle non-finite values.
Results may differ from the reference program's by a relative error of at most 0.007.
Values may be sent and summed in bfloat16 or wider, within the bound.
No kernel may reach another device: no remote copies, remote signals or barrier semaphores. Data moves between devices by JAX's collectives and lax.ppermute only.
A program may use at most 64 MiB of HBM per device.

```python
import jax
import jax.numpy as jnp
from jax import lax

NB = 160
E_LOC = 12
DEG = 4
REACH = 4
ER = 6
E = 192
NS = 256
N_ELEM = 16


def draw_neighbors(key, part):
    distance = jax.random.randint(jax.random.fold_in(key, 11), (E, 4), 1, REACH + 1)
    direction = jax.random.randint(jax.random.fold_in(key, 12), (E, 4), 0, 2) * 2 - 1
    itself = jnp.arange(E, dtype=jnp.int32)[:, None]
    others = jnp.mod(itself + distance * direction, E)
    return jnp.concatenate([itself, others], axis=1).astype(jnp.int32)


def draw_counts(key, part):
    base_count = NB * 3 // 5
    cap_elem = NB * 9 // 10
    budget = ER * (cap_elem - base_count)
    extra = jax.random.randint(jax.random.fold_in(key, 21), (E // ER, ER), 0, NB - base_count + 1)
    before = jnp.cumsum(extra, axis=1) - extra
    clipped = jnp.minimum(extra, jnp.maximum(budget - before, 0))
    first_extra = min(budget, NB - base_count)
    rest_extra = budget - first_extra
    others = max(ER - 1, 1)
    lanes = jnp.arange(ER, dtype=jnp.int32)
    spread = rest_extra // others + (lanes - 1 < rest_extra % others).astype(jnp.int32)
    forced = jnp.where(lanes == 0, first_extra, spread)
    block_ids = jnp.arange(E // ER, dtype=jnp.int32)
    is_first = block_ids * ER % E_LOC == 0
    final_extra = jnp.where(is_first[:, None], forced[None, :], clipped)
    return (base_count + final_extra).reshape(E).astype(jnp.int32)


def block_levels(own_key, shape, cuts, smallest, high):
    loudness, own = 1.0, jax.random.fold_in(own_key, 6)
    for axis_at, parts in cuts:
        draws = jnp.exp(jax.random.uniform(jax.random.fold_in(own, axis_at), (parts,), jnp.float32, smallest / len(cuts), high / len(cuts)))
        loudness = loudness * jnp.repeat(draws, shape[axis_at] // parts).reshape([-1 if axis == axis_at else 1 for axis in range(len(shape))])
    return loudness


def noise(rng, extent, width, bound, cuts=(), held_as=jnp.bfloat16):
    values = jax.random.normal(rng, extent, jnp.float32) * width
    if len(cuts) > 0:
        values = block_levels(rng, extent, cuts, -0.22, 0.18) * values
    return jnp.clip(values, min=-bound, max=bound).astype(held_as)


def setup_inputs(seed: int = 0) -> dict:
    key_list = jax.random.split(jax.random.key(seed), 6)
    orbitals = noise(key_list[0], (E, NB, NS), 1.0, 6.0, ((0, 32),))
    rotation = noise(key_list[1], (NS, NS), NS ** -0.5, 0.375)
    counts = draw_counts(jax.random.fold_in(key_list[5], 71), 0)
    neighbors = draw_neighbors(jax.random.fold_in(key_list[5], 71), 0)
    blocks = noise(key_list[4], (E, 5, NB, NB), (5 * NB) ** -0.5, 0.21875, ((0, 16),))
    return {"orbitals": orbitals, "rotation": rotation, "counts": counts, "neighbors": neighbors, "blocks": blocks}


center_shift = 0.2
half_span = 1.1


def reference(orbitals, rotation, counts, neighbors, blocks):
    total = orbitals.shape[0]
    flat = jnp.dot(orbitals.reshape(total * NB, NS), rotation, preferred_element_type=jnp.float32)
    flat = flat.reshape(total, NB, NS)
    row_mask = (jnp.arange(NB, dtype=jnp.int32)[None, :, None] < counts[:, None, None]).astype(jnp.float32)
    start = (flat * row_mask).astype(jnp.bfloat16)

    def chebyshev(current, previous, factor, with_prev):
        def one_slab(slab):
            lower = (slab * E_LOC).astype(jnp.int32)
            source = lax.dynamic_slice_in_dim(neighbors, lower, E_LOC, 0)
            local_blocks = lax.dynamic_slice_in_dim(blocks, lower, E_LOC, 0).astype(jnp.float32)
            local_mask = lax.dynamic_slice_in_dim(row_mask, lower, E_LOC, 0)
            gathered = current[source].astype(jnp.float32)
            image = jnp.einsum("ekij,ekjs->eis", local_blocks, gathered) * local_mask
            here = lax.dynamic_slice_in_dim(current, lower, E_LOC, 0).astype(jnp.float32)
            value = factor * (image - center_shift * here) / half_span
            if with_prev:
                value = value - lax.dynamic_slice_in_dim(previous, lower, E_LOC, 0).astype(jnp.float32)
            return value.astype(jnp.bfloat16)

        result = lax.map(one_slab, jnp.arange(N_ELEM, dtype=jnp.int32))
        return result.reshape(total, NB, NS)

    previous = start
    current = chebyshev(start, start, 1.0, False)
    for degree in range(DEG - 1):
        following = chebyshev(current, previous, 2.0, True)
        previous = current
        current = following
    return current
```

```python
import functools

import jax
import jax.numpy as jnp
from jax import lax
from jax.experimental import pallas as pl
from jax.experimental.pallas import tpu as pltpu
from jax.sharding import PartitionSpec as P

DEG = 4

center_shift = 0.2
half_span = 1.1

VMEM = pl.BlockSpec(memory_space=pltpu.VMEM)
SMEM = pl.BlockSpec(memory_space=pltpu.SMEM)
HBM = pl.BlockSpec(memory_space=pl.ANY)


def call(kernel, outs, ins, *args, scratch=(), out_specs=None, aliases=None, limit=16 << 20, flops=0, name=None):
    shapes = [jax.ShapeDtypeStruct(shape, jnp.bfloat16) for shape in outs]
    return pl.pallas_call(
        kernel,
        out_shape=shapes,
        in_specs=ins,
        out_specs=out_specs or [VMEM] * len(outs),
        scratch_shapes=list(scratch),
        input_output_aliases=aliases or {},
        compiler_params=pltpu.CompilerParams(vmem_limit_bytes=limit),
        cost_estimate=pl.CostEstimate(flops=flops, bytes_accessed=1 << 19, transcendentals=0),
        name=name,
    )(*args)


def rows_below(count, rows, lanes):
    return lax.broadcasted_iota(jnp.int32, (rows, lanes), 0) < count


def rotate_kernel(shards, orbitals, rotation, counts, *outs):
    me = lax.axis_index("state")
    elems, rows, states = orbitals.shape
    lanes = states // shards
    flat = orbitals[...].reshape(elems * rows, states)
    for k, out in enumerate(outs):
        at = lax.rem(me + k, shards) * lanes
        weights = rotation[:, pl.ds(pl.multiple_of(at, lanes), lanes)]
        turned = jnp.dot(flat, weights, preferred_element_type=jnp.float32).reshape(elems, rows, lanes)
        for e in range(elems):
            keep = rows_below(counts[me * elems + e], rows, lanes)
            out[e] = jnp.where(keep, turned[e], 0.0).astype(jnp.bfloat16)


def gather_kernel(shards, *refs):
    me = lax.axis_index("state")
    parts, groups, whole = refs[:shards], refs[shards : shards + 3], refs[-1]
    elems, width = parts[0].shape[0], groups[0].shape[0]
    for k, part in enumerate(parts):
        whole[pl.ds(lax.rem(me + shards - k, shards) * elems, elems)] = part[...]
    for g, group in enumerate(groups):
        group[...] = whole[g * width : (g + 1) * width]


def level_kernel(first, factor, with_prev, blocks, source, counts, before, here, after, *refs):
    if with_prev:
        previous, out, window = refs
    else:
        out, window = refs
    width, rows, lanes = here.shape
    for g, group in enumerate((before, here, after)):
        window[g * width : (g + 1) * width] = group[...]
    for e in range(width):
        image = jnp.zeros((rows, lanes), jnp.float32)
        for k in range(blocks.shape[1]):
            field = window[source[first + e, k]]
            image += jnp.dot(blocks[first + e, k], field, preferred_element_type=jnp.float32)
        image = jnp.where(rows_below(counts[first + e], rows, lanes), image, 0.0)
        value = factor * (image - center_shift * here[e].astype(jnp.float32)) / half_span
        if with_prev:
            value = value - previous[e].astype(jnp.float32)
        out[e] = value.astype(jnp.bfloat16)


def scatter_kernel(shards, *refs):
    me = lax.axis_index("state")
    groups, parts, whole = refs[:3], refs[3:-1], refs[-1]
    elems, width = parts[0].shape[0], groups[0].shape[0]
    for g, group in enumerate(groups):
        whole[g * width : (g + 1) * width] = group[...]
    for k, part in enumerate(parts):
        part[...] = whole[pl.ds(lax.rem(me + k, shards) * elems, elems)]


def join_kernel(shards, *refs):
    me = lax.axis_index("state")
    parts, out = refs[:shards], refs[shards]
    lanes = parts[0].shape[2]
    for k, part in enumerate(parts):
        at = lax.rem(me + shards - k, shards) * lanes
        out[:, :, pl.ds(pl.multiple_of(at, lanes), lanes)] = part[...]


def on_device(orbitals, rotation, counts, neighbors, blocks):
    row_elems, rows, states = orbitals.shape
    elems = counts.shape[0]
    shards = lax.axis_size("state")
    ring = lax.axis_size("elem")
    width = elems // 3
    lanes = states // shards
    group = (width, rows, lanes)

    def to_right(x):
        return lax.ppermute(x, "elem", [(i, (i + 1) % ring) for i in range(ring)])

    def to_left(x):
        return lax.ppermute(x, "elem", [(i, (i - 1) % ring) for i in range(ring)])

    def swapped(parts):
        return [parts[0]] + [
            lax.ppermute(part, "state", [(i, (i + k) % shards) for i in range(shards)])
            for k, part in enumerate(parts)
            if k > 0
        ]

    total = elems * ring
    mine = lax.axis_index("elem") * elems + jnp.arange(elems, dtype=jnp.int32)
    offset = jnp.mod(neighbors - mine[:, None] + width, total)
    source = offset + jnp.mod(jnp.arange(elems, dtype=jnp.int32), width)[:, None]

    part = (row_elems, rows, lanes)
    parts = call(
        functools.partial(rotate_kernel, shards),
        [part] * shards,
        [VMEM, VMEM, SMEM],
        orbitals,
        rotation,
        counts,
        name="rotate",
    )
    parts = swapped(parts)
    start = call(
        functools.partial(gather_kernel, shards),
        [group] * 3,
        [VMEM] * shards,
        *parts,
        scratch=[pltpu.VMEM((elems, rows, lanes), jnp.bfloat16)],
        name="gather",
    )

    def level(g, factor, before, here, after, previous=None):
        body = functools.partial(level_kernel, g * width, factor, previous is not None)
        args = [blocks, source, counts, before, here, after] + ([] if previous is None else [previous])
        return call(
            body,
            [group],
            [VMEM, SMEM, SMEM] + [VMEM] * (len(args) - 3),
            *args,
            scratch=[pltpu.VMEM((3 * width, rows, lanes), jnp.bfloat16)],
            flops=2 * width * blocks.shape[1] * rows * rows * lanes,
            name=("low", "middle", "high")[g],
        )[0]

    older, (low, middle, high) = (None, None, None), start
    for m in range(DEG):
        factor = 1.0 if m == 0 else 2.0
        from_left, from_right = to_right(high), to_left(low)
        newer = (
            level(0, factor, from_left, low, middle, older[0]),
            level(1, factor, low, middle, high, older[1]),
            level(2, factor, middle, high, from_right, older[2]),
        )
        older, (low, middle, high) = (low, middle, high), newer

    parts = call(
        functools.partial(scatter_kernel, shards),
        [part] * shards,
        [VMEM] * 3,
        low,
        middle,
        high,
        scratch=[pltpu.VMEM((elems, rows, lanes), jnp.bfloat16)],
        name="scatter",
    )
    parts = swapped(parts)
    return call(
        functools.partial(join_kernel, shards), [orbitals.shape], [VMEM] * shards, *parts, name="join"
    )[0]


def solution(mesh):
    in_specs = (
        P(("elem", "state"), None, None),
        P(),
        P("elem"),
        P("elem", None),
        P("elem", None, None, None),
    )
    out_specs = P(("elem", "state"), None, None)
    return jax.shard_map(on_device, mesh=mesh, in_specs=in_specs, out_specs=out_specs, check_vma=False)
```

```python
import functools

import jax
import jax.numpy as jnp
from jax import lax
from jax.experimental import pallas as pl
from jax.experimental.pallas import tpu as pltpu
from jax.sharding import PartitionSpec as P

DEG = 4
FULL = 128

center_shift = 0.2
half_span = 1.1

VMEM = pl.BlockSpec(memory_space=pltpu.VMEM)
HBM = pl.BlockSpec(memory_space=pltpu.HBM)
ANY = pl.BlockSpec(memory_space=pl.ANY)


def call(kernel, outs, ins, *args, out_specs=None, scratch=(), aliases=None, limit=4 << 20, flops=0, name=None):
    return pl.pallas_call(
        kernel,
        out_shape=outs,
        in_specs=ins,
        out_specs=out_specs or [VMEM] * len(outs),
        scratch_shapes=list(scratch),
        input_output_aliases=aliases or {},
        compiler_params=pltpu.CompilerParams(vmem_limit_bytes=limit),
        cost_estimate=pl.CostEstimate(flops=flops, bytes_accessed=1 << 20, transcendentals=0),
        name=name,
    )(*args)


def bf16(*shape):
    return jax.ShapeDtypeStruct(shape, jnp.bfloat16)


def rows_below(count, rows, lanes):
    return lax.broadcasted_iota(jnp.int32, (rows, lanes), 0) < count


def turn(shards, k, element, weights, count):
    rows, lanes = element.shape[0], weights.shape[1] // shards
    at = lax.rem(lax.axis_index("state") + k, shards) * lanes
    turned = jnp.dot(element, weights[:, pl.ds(pl.multiple_of(at, lanes), lanes)], preferred_element_type=jnp.float32)
    return jnp.where(rows_below(count, rows, lanes), turned, 0.0).astype(jnp.bfloat16)


def rotate_out_kernel(shards, orbitals, rotation, counts, *refs):
    outs, (held, weights, limits, sems) = refs[: shards - 1], refs[shards - 1 :]
    elems = orbitals.shape[0]
    me = lax.axis_index("state")
    copies = [
        pltpu.make_async_copy(rotation, weights, sems.at[0]),
        pltpu.make_async_copy(counts, limits, sems.at[1]),
    ]
    copies += [pltpu.make_async_copy(orbitals.at[e], held.at[e], sems.at[2 + e]) for e in range(elems)]
    for copy in copies:
        copy.start()
    copies[0].wait()
    copies[1].wait()
    for e in range(elems):
        copies[2 + e].wait()
        for k, out in enumerate(outs):
            out[e] = turn(shards, k + 1, held[e], weights, limits[me * elems + e])


def local_kernel(reach, total, shards, blocks, neighbors, counts, held, weights, kept, packed, source, limits, raw, scalars, sems):
    elems, couplings, rows, _ = blocks.shape
    copies = [pltpu.make_async_copy(blocks.at[e], raw.at[e], sems.at[e]) for e in range(elems)]
    more = [
        pltpu.make_async_copy(counts, scalars, sems.at[elems]),
        pltpu.make_async_copy(counts, limits, sems.at[elems + 1]),
    ]
    for copy in more + copies:
        copy.start()
    row = lax.broadcasted_iota(jnp.int32, neighbors.shape, 0)
    offset = neighbors[...] - (row + lax.axis_index("elem") * elems)
    offset = jnp.where(offset > reach, offset - total, jnp.where(offset < -reach, offset + total, offset))
    within = row
    for g in range(1, elems // reach):
        within = jnp.where(row >= g * reach, row - g * reach, within)
    source[...] = offset + within + reach
    for copy in more:
        copy.wait()
    mine = held.shape[0]
    for e in range(mine):
        kept[e] = turn(shards, 0, held[e], weights, scalars[lax.axis_index("state") * mine + e])
    for e in range(elems):
        copies[e].wait()
        for k in range(couplings):
            packed[e, :, k * FULL : (k + 1) * FULL] = raw[e, k, :, :FULL]
        packed[e, :, couplings * FULL :] = jnp.concatenate([raw[e, k, :, FULL:] for k in range(couplings)], axis=1)


def gather_kernel(shards, *refs):
    me = lax.axis_index("state")
    parts, groups, whole = refs[:shards], refs[shards : shards + 3], refs[-1]
    elems, width = parts[0].shape[0], groups[0].shape[0]
    for k, part in enumerate(parts):
        whole[pl.ds(lax.rem(me + shards - k, shards) * elems, elems)] = part[...]
    for g, group in enumerate(groups):
        group[...] = whole[g * width : (g + 1) * width]


def level_kernel(first, factor, with_prev, packed, source, limits, before, here, after, *refs):
    out, window = refs[-2:]
    width, rows, lanes = here.shape
    for g, group in enumerate((before, here, after)):
        window[g * width : (g + 1) * width] = group[...]
    places, ends = source[...], limits[...]
    for e in range(width):
        at = [places[first + e, k] for k in range(places.shape[1])]
        fields = [window[i, :FULL] for i in at] + [window[i, FULL:] for i in at]
        image = jnp.dot(packed[first + e], jnp.concatenate(fields, axis=0), preferred_element_type=jnp.float32)
        image = jnp.where(rows_below(ends[first + e], rows, lanes), image, 0.0)
        value = factor * (image - center_shift * here[e].astype(jnp.float32)) / half_span
        if with_prev:
            value = value - refs[0][e].astype(jnp.float32)
        out[e] = value.astype(jnp.bfloat16)


def scatter_kernel(shards, *refs):
    me = lax.axis_index("state")
    groups, parts, whole = refs[:3], refs[3:-1], refs[-1]
    elems, width = parts[0].shape[0], groups[0].shape[0]
    for g, group in enumerate(groups):
        whole[g * width : (g + 1) * width] = group[...]
    for k, part in enumerate(parts):
        part[...] = whole[pl.ds(lax.rem(me + k, shards) * elems, elems)]


def place(shards, k, part, out, sem):
    lanes = part.shape[2]
    at = lax.rem(lax.axis_index("state") + shards - k, shards) * lanes
    return pltpu.make_async_copy(part, out.at[:, :, pl.ds(pl.multiple_of(at, lanes), lanes)], sem)


def own_kernel(shards, part, out, sem):
    copy = place(shards, 0, part, out, sem)
    copy.start()
    copy.wait()


def others_kernel(shards, *refs):
    parts, out, sems = refs[: shards - 1], refs[-2], refs[-1]
    copies = [place(shards, k + 1, part, out, sems.at[k]) for k, part in enumerate(parts)]
    for copy in copies:
        copy.start()
    for copy in copies:
        copy.wait()


def on_device(orbitals, rotation, counts, neighbors, blocks):
    row_elems, rows, states = orbitals.shape
    elems, couplings = neighbors.shape
    orbitals, rotation, counts, blocks = (
        pltpu.with_memory_space_constraint(x, pltpu.HBM) for x in (orbitals, rotation, counts, blocks)
    )
    shards = lax.axis_size("state")
    ring = lax.axis_size("elem")
    width = elems // 3
    lanes = states // shards
    group, part = bf16(width, rows, lanes), bf16(row_elems, rows, lanes)
    whole = pltpu.VMEM((elems, rows, lanes), jnp.bfloat16)
    scalars = pltpu.SMEM(counts.shape, jnp.int32)
    dma = pltpu.SemaphoreType.DMA

    def to_right(x):
        return lax.ppermute(x, "elem", [(i, (i + 1) % ring) for i in range(ring)])

    def to_left(x):
        return lax.ppermute(x, "elem", [(i, (i - 1) % ring) for i in range(ring)])

    def swapped(parts):
        return [
            lax.ppermute(part, "state", [(i, (i + k + 1) % shards) for i in range(shards)])
            for k, part in enumerate(parts)
        ]

    *parts, held, weights = call(
        functools.partial(rotate_out_kernel, shards),
        [part] * (shards - 1) + [bf16(*orbitals.shape), bf16(*rotation.shape)],
        [HBM] * 3,
        orbitals,
        rotation,
        counts,
        scratch=[scalars, dma((row_elems + 2,))],
        name="rotate_out",
    )
    arrived = swapped(parts)
    kept, packed, source, limits = call(
        functools.partial(local_kernel, width, elems * ring, shards),
        [
            part,
            bf16(elems, rows, couplings * rows),
            jax.ShapeDtypeStruct(neighbors.shape, jnp.int32),
            jax.ShapeDtypeStruct(counts.shape, jnp.int32),
        ],
        [HBM, VMEM, HBM, VMEM, VMEM],
        blocks,
        neighbors,
        counts,
        held,
        weights,
        scratch=[pltpu.VMEM(blocks.shape, jnp.bfloat16), scalars, dma((elems + 2,))],
        limit=16 << 20,
        name="local",
    )
    low, middle, high = call(
        functools.partial(drop_input, functools.partial(gather_kernel, shards), shards),
        [group] * 3,
        [VMEM] * shards + [ANY],
        kept,
        *arrived,
        packed,
        scratch=[whole],
        name="gather",
    )

    def level(g, m, before, here, after, previous, behind=None):
        body = functools.partial(level_kernel, g * width, 1.0 if m == 1 else 2.0, previous is not None)
        if behind is not None:
            body = functools.partial(drop_input, body, 6 + (previous is not None))
        args = [packed, source, limits, before, here, after] + ([] if previous is None else [previous])
        specs = [VMEM] * len(args)
        if behind is not None:
            args, specs = args + [behind], specs + [ANY]
        return call(
            body,
            [group],
            specs,
            *args,
            scratch=[pltpu.VMEM((3 * width, rows, lanes), jnp.bfloat16)],
            flops=2 * width * couplings * rows * rows * lanes,
            name=("low", "middle", "high")[g] + str(m),
        )[0]

    older = (None, None, None)
    from_right, from_left = to_left(low), to_right(high)
    for m in range(1, DEG + 1):
        if m % 2:
            new_high = level(2, m, middle, high, from_right, older[2])
            right_halo = to_right(new_high) if m < DEG else None
            new_low = level(0, m, from_left, low, middle, older[0], new_high)
            left_halo = to_left(new_low) if m < DEG else None
        else:
            new_low = level(0, m, from_left, low, middle, older[0])
            left_halo = to_left(new_low) if m < DEG else None
            new_high = level(2, m, middle, high, from_right, older[2], new_low)
            right_halo = to_right(new_high) if m < DEG else None
        new_middle = level(1, m, low, middle, high, older[1])
        from_left, from_right = right_halo, left_halo
        older, (low, middle, high) = (low, middle, high), (new_low, new_middle, new_high)

    kept, *parts = call(
        functools.partial(scatter_kernel, shards),
        [part] * shards,
        [VMEM] * 3,
        low,
        middle,
        high,
        scratch=[whole],
        name="scatter",
    )
    arrived = swapped(parts)
    out = call(
        functools.partial(own_kernel, shards),
        [bf16(*orbitals.shape)],
        [VMEM],
        kept,
        out_specs=[HBM],
        scratch=[dma],
        name="own",
    )[0]
    return call(
        functools.partial(drop_input, functools.partial(others_kernel, shards), shards - 1),
        [bf16(*orbitals.shape)],
        [VMEM] * (shards - 1) + [HBM],
        *arrived,
        out,
        out_specs=[HBM],
        scratch=[dma((shards - 1,))],
        aliases={shards - 1: 0},
        name="others",
    )[0]


def drop_input(body, at, *refs):
    body(*refs[:at], *refs[at + 1 :])


def solution(mesh):
    in_specs = (
        P(("elem", "state"), None, None),
        P(),
        P("elem"),
        P("elem", None),
        P("elem", None, None, None),
    )
    out_specs = P(("elem", "state"), None, None)
    return jax.shard_map(on_device, mesh=mesh, in_specs=in_specs, out_specs=out_specs, check_vma=False)
```

```python
import functools

import jax
import jax.numpy as jnp
from jax import lax
from jax.experimental import pallas as pl
from jax.experimental.pallas import tpu as pltpu
from jax.sharding import PartitionSpec as P

DEG = 4
FULL = 128
LONG = 20 * 10**9

center_shift = 0.2
half_span = 1.1

VMEM = pl.BlockSpec(memory_space=pltpu.VMEM)
HBM = pl.BlockSpec(memory_space=pltpu.HBM)
ANY = pl.BlockSpec(memory_space=pl.ANY)


def call(kernel, outs, ins, *args, out_specs=None, scratch=(), aliases=None, limit=4 << 20, flops=0, name=None):
    return pl.pallas_call(
        kernel,
        out_shape=outs,
        in_specs=ins,
        out_specs=out_specs or [VMEM] * len(outs),
        scratch_shapes=list(scratch),
        input_output_aliases=aliases or {},
        compiler_params=pltpu.CompilerParams(vmem_limit_bytes=limit),
        cost_estimate=pl.CostEstimate(flops=flops, bytes_accessed=1024, transcendentals=0),
        name=name,
    )(*args)


def bf16(*shape):
    return jax.ShapeDtypeStruct(shape, jnp.bfloat16)


def without(body, at, *refs):
    body(*refs[:at], *refs[at + 1 :])


def flipped(shards):
    return lax.axis_index("state") == 1 if shards == 2 else False


def choose(flip, yes, no):
    return no if flip is False else jnp.where(flip, yes, no)


def rows_below(count, rows, lanes):
    return lax.broadcasted_iota(jnp.int32, (rows, lanes), 0) < count


def turn(shards, k, element, weights, count):
    rows, lanes = element.shape[0], weights.shape[1] // shards
    at = lax.rem(lax.axis_index("state") + k, shards) * lanes
    turned = jnp.dot(element, weights[:, pl.ds(pl.multiple_of(at, lanes), lanes)], preferred_element_type=jnp.float32)
    return jnp.where(rows_below(count, rows, lanes), turned, 0.0).astype(jnp.bfloat16)


def rotate_out_kernel(shards, reach, orbitals, rotation, counts, *refs):
    outs, (held, weights, limits, scalars, sems) = refs[:-5], refs[-5:]
    elems = orbitals.shape[0]
    me, flip = lax.axis_index("state"), flipped(shards)
    copies = [
        pltpu.make_async_copy(rotation, weights, sems.at[0]),
        pltpu.make_async_copy(counts, scalars, sems.at[1]),
        pltpu.make_async_copy(counts, limits, sems.at[2]),
    ]
    copies += [pltpu.make_async_copy(orbitals.at[e], held.at[e], sems.at[3 + e]) for e in range(elems)]
    for copy in copies:
        copy.start()
    copies[0].wait()
    copies[1].wait()
    for e in range(elems):
        copies[3 + e].wait()
        for k in range(shards - 1):
            spot = choose(flip, (e + reach) % elems, e)
            outs[k][spot] = turn(shards, k + 1, held[e], weights, scalars[me * elems + e])
    if shards == 2:
        outs[1][...] = outs[0][:reach]
    copies[2].wait()


def rotate_in_kernel(shards, reach, held, weights, limits, *outs):
    me, flip = lax.axis_index("state"), flipped(shards)
    elems = held.shape[0]
    ends = limits[...]
    spots = [(out, e) for out in outs for e in range(out.shape[0])]
    for spot, (out, at) in enumerate(spots):
        e = choose(flip, (spot + elems - reach) % elems, spot)
        count = ends[spot]
        for shard in range(shards):
            here = (spot + elems - reach) % elems if shard == 1 and flip is not False else spot
            count = jnp.where(me == shard, ends[shard * elems + here], count)
        out[at] = turn(shards, 0, held[e], weights, count)


def local_kernel(total, shards, reach, blocks, neighbors, limits, *refs):
    packed, (table, raw, beside, sems) = refs[:-4], refs[-4:]
    elems, couplings, _, _ = blocks.shape
    flip, groups = flipped(shards), elems // reach
    spots = [choose(flip, elems - (g + 1) * reach, g * reach) + e for g in range(groups) for e in range(reach)]
    copies = [pltpu.make_async_copy(blocks.at[e], raw.at[i], sems.at[i]) for i, e in enumerate(spots)]
    neighbor_copy = pltpu.make_async_copy(neighbors, beside, sems.at[elems])
    neighbor_copy.start()
    for copy in copies:
        copy.start()
    neighbor_copy.wait()
    column = lax.broadcasted_iota(jnp.int32, beside.shape, 1)
    offset = beside[...] - (column + lax.axis_index("elem") * elems)
    offset = jnp.where(offset > reach, offset - total, jnp.where(offset < -reach, offset + total, offset))
    place = offset + (column - sum(jnp.where(column >= g * reach, reach, 0) for g in range(1, groups))) + reach
    past = sum(jnp.where(place >= g * reach, reach, 0) for g in range(1, groups))
    place = choose(flip, place + (elems - reach) - 2 * past, place)
    ends = limits[...].reshape(1, elems)

    def mirrored(x):
        parts = [x[:, g * reach : (g + 1) * reach] for g in reversed(range(groups))]
        return choose(flip, jnp.concatenate(parts, axis=1), x)

    table[:couplings] = mirrored(place)
    table[couplings:] = mirrored(ends)
    for i in range(elems):
        out, e = packed[i // reach], i % reach
        copies[i].wait()
        for k in range(couplings):
            out[e, :, k * FULL : (k + 1) * FULL] = raw[i, k, :, :FULL]
        tail = [raw[i, k, :, FULL:] for k in range(couplings)]
        out[e, :, couplings * FULL :] = jnp.concatenate(tail, axis=1)


def pair_kernel(reach, arrived, half, far, middle):
    flip, share = flipped(2), half.shape[0]
    far[...] = arrived[:reach]
    middle[pl.ds(choose(flip, share, 0), share)] = half[...]
    middle[pl.ds(choose(flip, 0, share), share)] = arrived[reach:]


def gather_kernel(shards, *refs):
    me = lax.axis_index("state")
    parts, groups, whole = refs[:shards], refs[shards : shards + 3], refs[-1]
    elems, width = parts[0].shape[0], groups[0].shape[0]
    for k, part in enumerate(parts):
        whole[pl.ds(lax.rem(me + shards - k, shards) * elems, elems)] = part[...]
    for g, group in enumerate(groups):
        group[...] = whole[g * width : (g + 1) * width]


def level_kernel(first, factor, with_prev, packed, table, before, here, after, *refs):
    refs, out, window = list(refs[:-2]), refs[-2], refs[-1]
    previous = refs.pop(0) if with_prev else None
    width, rows, lanes = here.shape
    for g, group in enumerate((before, here, after)):
        window[g * width : (g + 1) * width] = group[...]
    places = table[...]
    couplings = places.shape[0] - 1
    for e in range(width):
        at = [places[k, first + e] for k in range(couplings)]
        fields = [window[i, :FULL] for i in at] + [window[i, FULL:] for i in at]
        image = jnp.dot(packed[e], jnp.concatenate(fields, axis=0), preferred_element_type=jnp.float32)
        image = jnp.where(rows_below(places[couplings, first + e], rows, lanes), image, 0.0)
        value = factor * (image - center_shift * here[e].astype(jnp.float32)) / half_span
        if with_prev:
            value = value - previous[e].astype(jnp.float32)
        out[e] = value.astype(jnp.bfloat16)
    if refs:
        share = out.shape[0] - width
        out[width:] = refs[0][pl.ds(choose(flipped(2), 0, width - share), share)]


def scatter_kernel(shards, *refs):
    me = lax.axis_index("state")
    groups, parts, whole = refs[:3], refs[3:-1], refs[-1]
    elems, width = parts[0].shape[0], groups[0].shape[0]
    for g, group in enumerate(groups):
        whole[g * width : (g + 1) * width] = group[...]
    for k, part in enumerate(parts):
        part[...] = whole[pl.ds(lax.rem(me + k, shards) * elems, elems)]


def place(shards, k, first, part, out, sem):
    elems, _, lanes = part.shape
    at = lax.rem(lax.axis_index("state") + shards - k, shards) * lanes
    return pltpu.make_async_copy(part, out.at[pl.ds(first, elems), :, pl.ds(pl.multiple_of(at, lanes), lanes)], sem)


def run(copies):
    for copy in copies:
        copy.start()
    for copy in copies:
        copy.wait()


def rows_copies(k, near, half, out, sems):
    flip, share, width = flipped(2), half.shape[0], near.shape[0]
    return [
        place(2, k, choose(flip, share, 0), near, out, sems.at[0]),
        place(2, k, choose(flip, 0, width), half, out, sems.at[1]),
    ]


def own_kernel(near, middle, out, sems):
    share = out.shape[0] - near.shape[0]
    run(rows_copies(0, near, middle.at[pl.ds(choose(flipped(2), share, 0), share)], out, sems))


def others_kernel(width, part, out, sems):
    run(rows_copies(1, part.at[:width], part.at[width:], out, sems))


def join_kernel(shards, *refs):
    parts, out, sems = refs[:shards], refs[-2], refs[-1]
    run([place(shards, k, 0, part, out, sems.at[k]) for k, part in enumerate(parts)])


def on_device(orbitals, rotation, counts, neighbors, blocks):
    row_elems, rows, states = orbitals.shape
    elems, couplings = neighbors.shape
    orbitals, rotation, counts, neighbors, blocks = (
        pltpu.with_memory_space_constraint(x, pltpu.HBM) for x in (orbitals, rotation, counts, neighbors.T, blocks)
    )
    shards = lax.axis_size("state")
    ring = lax.axis_size("elem")
    width = elems // 3
    lanes = states // shards
    group, part = bf16(width, rows, lanes), bf16(row_elems, rows, lanes)
    half = bf16(row_elems - width, rows, lanes)
    whole = pltpu.VMEM((elems, rows, lanes), jnp.bfloat16)
    scalars = pltpu.SMEM(counts.shape, jnp.int32)
    dma = pltpu.SemaphoreType.DMA
    pair = shards == 2

    def shifted(x, step, across=False):
        moves = []
        for i in range(ring):
            for j in range(shards):
                to = (i + (-step if pair and j == 1 else step)) % ring
                moves.append((i * shards + j, to * shards + (1 - j if across else j)))
        return lax.ppermute(x, ("elem", "state"), moves)

    def to_far_of_neighbor(x):
        return shifted(x, -1)

    def to_near_of_neighbor(x):
        return shifted(x, 1)

    def swapped(parts):
        return [
            lax.ppermute(x, "state", [(i, (i + k + 1) % shards) for i in range(shards)]) for k, x in enumerate(parts)
        ]

    *parts, held, weights, limits = call(
        functools.partial(rotate_out_kernel, shards, width),
        [part] * (shards - 1)
        + [group] * pair
        + [bf16(*orbitals.shape), bf16(*rotation.shape), jax.ShapeDtypeStruct(counts.shape, jnp.int32)],
        [HBM] * 3,
        orbitals,
        rotation,
        counts,
        scratch=[scalars, dma((row_elems + 3,))],
        name="rotate_out",
    )
    arrived = swapped(parts[: shards - 1])
    if pair:
        near_halo = shifted(parts[1], -1, across=True)
    kept = call(
        functools.partial(rotate_in_kernel, shards, width),
        [group, half] if pair else [part],
        [VMEM] * 3,
        held,
        weights,
        limits,
        name="rotate_in",
    )
    if pair:
        far_halo = to_far_of_neighbor(kept[0])
    *packed, table = call(
        functools.partial(without, functools.partial(local_kernel, elems * ring, shards, width), 3),
        [bf16(width, rows, couplings * rows)] * 3 + [jax.ShapeDtypeStruct((couplings + 1, elems), jnp.int32)],
        [HBM, HBM, VMEM, ANY],
        blocks,
        neighbors,
        limits,
        kept[0],
        scratch=[pltpu.VMEM(blocks.shape, jnp.bfloat16), pltpu.VMEM(neighbors.shape, jnp.int32), dma((elems + 1,))],
        limit=16 << 20,
        name="local",
    )
    if pair:
        near = kept[0]
        far, middle = call(
            functools.partial(without, functools.partial(pair_kernel, width), 2),
            [group] * 2,
            [VMEM, VMEM, ANY],
            *arrived,
            kept[1],
            table,
            name="gather",
        )
    else:
        near, middle, far = call(
            functools.partial(without, functools.partial(gather_kernel, shards), shards),
            [group] * 3,
            [VMEM] * shards + [ANY],
            *kept,
            *arrived,
            table,
            scratch=[whole],
            name="gather",
        )
        near_halo, far_halo = to_near_of_neighbor(far), to_far_of_neighbor(near)

    def level(g, m, before, here, after, previous, leaving=None, behind=None, flops=0):
        body = functools.partial(level_kernel, g * width, 1.0 if m == 1 else 2.0, previous is not None)
        args = [packed[g], table, before, here, after] + [x for x in (previous, leaving) if x is not None]
        specs = [VMEM] * len(args)
        if behind is not None:
            body = functools.partial(without, body, len(args))
            args, specs = args + [behind], specs + [ANY]
        return call(
            body,
            [group if leaving is None else part],
            specs,
            *args,
            scratch=[pltpu.VMEM((3 * width, rows, lanes), jnp.bfloat16)],
            flops=flops,
            name=("near", "middle", "far")[g] + str(m),
        )[0]

    older = (None, None, None)
    for m in range(1, DEG + 1):
        last = m == DEG
        if last:
            new_middle = level(1, m, near, middle, far, older[1])
        if m % 2:
            new_near = level(0, m, near_halo, near, middle, older[0])
            next_far_halo = to_far_of_neighbor(new_near)
            new_far = level(2, m, middle, far, far_halo, older[2], behind=new_near)
            next_near_halo = to_near_of_neighbor(new_far)
        else:
            new_far = level(2, m, middle, far, far_halo, older[2], new_middle if last and pair else None)
            if last and pair:
                arrived = swapped([new_far])[0]
            else:
                next_near_halo = to_near_of_neighbor(new_far)
            new_near = level(0, m, near_halo, near, middle, older[0], behind=None if last else new_far, flops=LONG * last)
            if not last:
                next_far_halo = to_far_of_neighbor(new_near)
        if not last:
            new_middle = level(1, m, near, middle, far, older[1])
            near_halo, far_halo = next_near_halo, next_far_halo
        older, (near, middle, far) = (near, middle, far), (new_near, new_middle, new_far)

    whole_out = [bf16(*orbitals.shape)]
    if pair:
        out = call(
            own_kernel, whole_out, [VMEM] * 2, near, middle, out_specs=[HBM], scratch=[dma((2,))], name="own"
        )[0]
        return call(
            functools.partial(without, functools.partial(others_kernel, width), 1),
            whole_out,
            [VMEM, HBM],
            arrived,
            out,
            out_specs=[HBM],
            scratch=[dma((2,))],
            aliases={1: 0},
            name="others",
        )[0]
    kept, *parts = call(
        functools.partial(scatter_kernel, shards),
        [part] * shards,
        [VMEM] * 3,
        near,
        middle,
        far,
        scratch=[whole],
        name="scatter",
    )
    return call(
        functools.partial(join_kernel, shards),
        whole_out,
        [VMEM] * shards,
        kept,
        *swapped(parts),
        out_specs=[HBM],
        scratch=[dma((shards,))],
        name="join",
    )[0]


def solution(mesh):
    in_specs = (
        P(("elem", "state"), None, None),
        P(),
        P("elem"),
        P("elem", None),
        P("elem", None, None, None),
    )
    out_specs = P(("elem", "state"), None, None)
    return jax.shard_map(on_device, mesh=mesh, in_specs=in_specs, out_specs=out_specs, check_vma=False)
```

```python
import functools

import jax
import jax.numpy as jnp
from jax import lax
from jax.experimental import pallas as pl
from jax.experimental.pallas import tpu as pltpu
from jax.sharding import PartitionSpec as P

DEG = 4
FULL = 128
LONG = 20 * 10**9

center_shift = 0.2
half_span = 1.1

VMEM = pl.BlockSpec(memory_space=pltpu.VMEM)
HBM = pl.BlockSpec(memory_space=pltpu.HBM)
ANY = pl.BlockSpec(memory_space=pl.ANY)


def call(kernel, outs, ins, *args, out_specs=None, scratch=(), aliases=None, limit=4 << 20, flops=0, name=None):
    return pl.pallas_call(
        kernel,
        out_shape=outs,
        in_specs=ins,
        out_specs=out_specs or [VMEM] * len(outs),
        scratch_shapes=list(scratch),
        input_output_aliases=aliases or {},
        compiler_params=pltpu.CompilerParams(vmem_limit_bytes=limit),
        cost_estimate=pl.CostEstimate(flops=flops, bytes_accessed=1024, transcendentals=0),
        name=name,
    )(*args)


def bf16(*shape):
    return jax.ShapeDtypeStruct(shape, jnp.bfloat16)


def without(body, at, *refs):
    body(*refs[:at], *refs[at + 1 :])


def flipped(shards):
    return lax.axis_index("state") == 1 if shards == 2 else False


def choose(flip, yes, no):
    return no if flip is False else jnp.where(flip, yes, no)


def rows_below(count, rows, lanes):
    return lax.broadcasted_iota(jnp.int32, (rows, lanes), 0) < count


def turn(shards, k, element, weights, count):
    rows, lanes = element.shape[0], weights.shape[1] // shards
    at = lax.rem(lax.axis_index("state") + k, shards) * lanes
    turned = jnp.dot(element, weights[:, pl.ds(pl.multiple_of(at, lanes), lanes)], preferred_element_type=jnp.float32)
    return jnp.where(rows_below(count, rows, lanes), turned, 0.0).astype(jnp.bfloat16)


def fetch_kernel(shards, reach, orbitals, rotation, counts, neighbors, *refs):
    outs, (held, weights, limits, beside, scalars, sems) = refs[:-6], refs[-6:]
    elems = orbitals.shape[0]
    me, flip = lax.axis_index("state"), flipped(shards)
    copies = [
        pltpu.make_async_copy(source, target, sems.at[i])
        for i, (source, target) in enumerate(
            [(rotation, weights), (counts, scalars), (orbitals, held), (counts, limits), (neighbors, beside)]
        )
    ]
    for copy in copies:
        copy.start()
    for copy in copies[:3]:
        copy.wait()
    first = reach if shards == 2 else 0
    for k, out in enumerate(outs):
        for at in range(out.shape[0]):
            e = choose(flip, (first + at + elems - reach) % elems, first + at)
            out[at] = turn(shards, k + 1, held[e], weights, scalars[me * elems + e])
    for copy in copies[3:]:
        copy.wait()


def rotate_kernel(shards, reach, k, held, weights, limits, *outs):
    me, flip = lax.axis_index("state"), flipped(shards)
    elems = held.shape[0]
    ends = limits[...]
    spots = [(out, e) for out in outs for e in range(out.shape[0])]
    for spot, (out, at) in enumerate(spots):
        e = choose(flip, (spot + elems - reach) % elems, spot)
        count = ends[spot]
        for shard in range(shards):
            here = (spot + elems - reach) % elems if shard == 1 and flip is not False else spot
            count = jnp.where(me == shard, ends[shard * elems + here], count)
        out[at] = turn(shards, k, held[e], weights, count)


def table_kernel(total, shards, reach, beside, limits, table):
    couplings, elems = beside.shape
    flip, groups = flipped(shards), elems // reach
    column = lax.broadcasted_iota(jnp.int32, beside.shape, 1)
    offset = beside[...] - (column + lax.axis_index("elem") * elems)
    offset = jnp.where(offset > reach, offset - total, jnp.where(offset < -reach, offset + total, offset))
    place = offset + (column - sum(jnp.where(column >= g * reach, reach, 0) for g in range(1, groups))) + reach
    past = sum(jnp.where(place >= g * reach, reach, 0) for g in range(1, groups))
    place = choose(flip, place + (elems - reach) - 2 * past, place)
    ends = limits[...].reshape(1, elems)

    def mirrored(x):
        parts = [x[:, g * reach : (g + 1) * reach] for g in reversed(range(groups))]
        return choose(flip, jnp.concatenate(parts, axis=1), x)

    table[:couplings] = mirrored(place)
    table[couplings:] = mirrored(ends)


def pack_kernel(shards, group, blocks, packed):
    elems, couplings, _, _ = blocks.shape
    width = packed.shape[0]
    first = choose(flipped(shards), elems - (group + 1) * width, group * width)
    for e in range(width):
        for k in range(couplings):
            packed[e, :, k * FULL : (k + 1) * FULL] = blocks[first + e, k, :, :FULL]
        tail = [blocks[first + e, k, :, FULL:] for k in range(couplings)]
        packed[e, :, couplings * FULL :] = jnp.concatenate(tail, axis=1)


def middle_kernel(half, arrived, leaving, middle, copied):
    flip, share = flipped(2), half.shape[0]
    copied[...] = leaving[...]
    middle[pl.ds(choose(flip, share, 0), share)] = half[...]
    middle[pl.ds(choose(flip, 0, share), share)] = arrived[...]


def gather_kernel(shards, *refs):
    me = lax.axis_index("state")
    parts, groups, whole = refs[:shards], refs[shards : shards + 3], refs[-1]
    elems, width = parts[0].shape[0], groups[0].shape[0]
    for k, part in enumerate(parts):
        whole[pl.ds(lax.rem(me + shards - k, shards) * elems, elems)] = part[...]
    for g, group in enumerate(groups):
        group[...] = whole[g * width : (g + 1) * width]


def level_kernel(first, factor, with_prev, packed, table, before, here, after, *refs):
    refs, out, window = list(refs[:-2]), refs[-2], refs[-1]
    previous = refs.pop(0) if with_prev else None
    width, rows, lanes = here.shape
    for g, group in enumerate((before, here, after)):
        window[g * width : (g + 1) * width] = group[...]
    places = table[...]
    couplings = places.shape[0] - 1
    for e in range(width):
        at = [places[k, first + e] for k in range(couplings)]
        fields = [window[i, :FULL] for i in at] + [window[i, FULL:] for i in at]
        image = jnp.dot(packed[e], jnp.concatenate(fields, axis=0), preferred_element_type=jnp.float32)
        image = jnp.where(rows_below(places[couplings, first + e], rows, lanes), image, 0.0)
        value = factor * (image - center_shift * here[e].astype(jnp.float32)) / half_span
        if with_prev:
            value = value - previous[e].astype(jnp.float32)
        out[e] = value.astype(jnp.bfloat16)
    if refs:
        share = out.shape[0] - width
        out[width:] = refs[0][pl.ds(choose(flipped(2), 0, width - share), share)]


def scatter_kernel(shards, *refs):
    me = lax.axis_index("state")
    groups, parts, whole = refs[:3], refs[3:-1], refs[-1]
    elems, width = parts[0].shape[0], groups[0].shape[0]
    for g, group in enumerate(groups):
        whole[g * width : (g + 1) * width] = group[...]
    for k, part in enumerate(parts):
        part[...] = whole[pl.ds(lax.rem(me + k, shards) * elems, elems)]


def place(shards, k, first, part, out, sem):
    elems, _, lanes = part.shape
    at = lax.rem(lax.axis_index("state") + shards - k, shards) * lanes
    return pltpu.make_async_copy(part, out.at[pl.ds(first, elems), :, pl.ds(pl.multiple_of(at, lanes), lanes)], sem)


def run(copies):
    for copy in copies:
        copy.start()
    for copy in copies:
        copy.wait()


def rows_copies(k, near, half, out, sems):
    flip, share, width = flipped(2), half.shape[0], near.shape[0]
    return [
        place(2, k, choose(flip, share, 0), near, out, sems.at[0]),
        place(2, k, choose(flip, 0, width), half, out, sems.at[1]),
    ]


def own_kernel(near, middle, out, sems):
    share = out.shape[0] - near.shape[0]
    run(rows_copies(0, near, middle.at[pl.ds(choose(flipped(2), share, 0), share)], out, sems))


def others_kernel(width, part, out, sems):
    run(rows_copies(1, part.at[:width], part.at[width:], out, sems))


def join_kernel(shards, *refs):
    parts, out, sems = refs[:shards], refs[-2], refs[-1]
    run([place(shards, k, 0, part, out, sems.at[k]) for k, part in enumerate(parts)])


def on_device(orbitals, rotation, counts, neighbors, blocks):
    row_elems, rows, states = orbitals.shape
    elems, couplings = neighbors.shape
    inputs = [
        pltpu.with_memory_space_constraint(x, pltpu.HBM) for x in (orbitals, rotation, counts, neighbors.T)
    ]
    shards = lax.axis_size("state")
    ring = lax.axis_size("elem")
    width = elems // 3
    lanes = states // shards
    group, part = bf16(width, rows, lanes), bf16(row_elems, rows, lanes)
    half = bf16(row_elems - width, rows, lanes)
    whole = pltpu.VMEM((elems, rows, lanes), jnp.bfloat16)
    scalars = pltpu.SMEM(counts.shape, jnp.int32)
    dma = pltpu.SemaphoreType.DMA
    pair = shards == 2

    def shifted(x, step, across=False):
        moves = []
        for i in range(ring):
            for j in range(shards):
                to = (i + (-step if pair and j == 1 else step)) % ring
                moves.append((i * shards + j, to * shards + (1 - j if across else j)))
        return lax.ppermute(x, ("elem", "state"), moves)

    def to_far_of_neighbor(x):
        return shifted(x, -1)

    def to_near_of_neighbor(x):
        return shifted(x, 1)

    def swapped(parts):
        return [
            lax.ppermute(x, "state", [(i, (i + k + 1) % shards) for i in range(shards)]) for k, x in enumerate(parts)
        ]

    *parts, held, weights, limits, beside = call(
        functools.partial(fetch_kernel, shards, width),
        ([half] if pair else [part] * (shards - 1)) + [jax.ShapeDtypeStruct(x.shape, x.dtype) for x in inputs],
        [HBM] * len(inputs),
        *inputs,
        scratch=[scalars, dma((5,))],
        flops=LONG,
        name="fetch",
    )
    if pair:
        arrived_half = swapped(parts)[0]
        leaving = call(
            functools.partial(rotate_kernel, shards, width, 1), [group], [VMEM] * 3, held, weights, limits, name="rotate_out"
        )[0]
        near_halo = shifted(leaving, -1, across=True)
        kept = call(
            functools.partial(rotate_kernel, shards, width, 0),
            [group, half],
            [VMEM] * 3,
            held,
            weights,
            limits,
            name="rotate_in",
        )
        far_halo = to_far_of_neighbor(kept[0])
        middle, leaving = call(
            middle_kernel, [group] * 2, [VMEM] * 3, kept[1], arrived_half, leaving, name="gather"
        )
        far = swapped([leaving])[0]
    else:
        arrived = swapped(parts)
        kept = call(
            functools.partial(rotate_kernel, shards, width, 0), [part], [VMEM] * 3, held, weights, limits, name="rotate_in"
        )
    table = call(
        functools.partial(without, functools.partial(table_kernel, elems * ring, shards, width), 2),
        [jax.ShapeDtypeStruct((couplings + 1, elems), jnp.int32)],
        [VMEM, VMEM, ANY],
        beside,
        limits,
        kept[0],
        name="table",
    )[0]

    def pack(g, behind):
        return call(
            functools.partial(without, functools.partial(pack_kernel, shards, g), 1),
            [bf16(width, rows, couplings * rows)],
            [VMEM, ANY],
            blocks,
            behind,
            name="pack",
        )[0]

    packed = {0: pack(0, table)}
    if pair:
        near = kept[0]
    else:
        near, middle, far = call(
            functools.partial(without, functools.partial(gather_kernel, shards), shards),
            [group] * 3,
            [VMEM] * shards + [ANY],
            *kept,
            *arrived,
            packed[0],
            scratch=[whole],
            name="gather",
        )
        near_halo, far_halo = to_near_of_neighbor(far), to_far_of_neighbor(near)

    def level(g, m, before, here, after, previous, leaving=None, behind=None, flops=0):
        body = functools.partial(level_kernel, g * width, 1.0 if m == 1 else 2.0, previous is not None)
        args = [packed[g], table, before, here, after] + [x for x in (previous, leaving) if x is not None]
        specs = [VMEM] * len(args)
        if behind is not None:
            body = functools.partial(without, body, len(args))
            args, specs = args + [behind], specs + [ANY]
        return call(
            body,
            [group if leaving is None else part],
            specs,
            *args,
            scratch=[pltpu.VMEM((3 * width, rows, lanes), jnp.bfloat16)],
            flops=flops,
            name=("near", "middle", "far")[g] + str(m),
        )[0]

    older = (None, None, None)
    for m in range(1, DEG + 1):
        last = m == DEG
        if last:
            new_middle = level(1, m, near, middle, far, older[1])
        if m % 2:
            new_near = level(0, m, near_halo, near, middle, older[0])
            next_far_halo = to_far_of_neighbor(new_near)
            if m == 1:
                packed[2] = pack(2, new_near)
            new_far = level(2, m, middle, far, far_halo, older[2], behind=new_near)
            next_near_halo = to_near_of_neighbor(new_far)
        else:
            new_far = level(2, m, middle, far, far_halo, older[2], new_middle if last and pair else None)
            if last and pair:
                arrived = swapped([new_far])[0]
            else:
                next_near_halo = to_near_of_neighbor(new_far)
            new_near = level(0, m, near_halo, near, middle, older[0], behind=None if last else new_far, flops=LONG * last)
            if not last:
                next_far_halo = to_far_of_neighbor(new_near)
        if m == 1:
            packed[1] = pack(1, new_far)
        if not last:
            new_middle = level(1, m, near, middle, far, older[1])
            near_halo, far_halo = next_near_halo, next_far_halo
        older, (near, middle, far) = (near, middle, far), (new_near, new_middle, new_far)

    whole_out = [bf16(*orbitals.shape)]
    if pair:
        out = call(
            own_kernel, whole_out, [VMEM] * 2, near, middle, out_specs=[HBM], scratch=[dma((2,))], name="own"
        )[0]
        return call(
            functools.partial(without, functools.partial(others_kernel, width), 1),
            whole_out,
            [VMEM, HBM],
            arrived,
            out,
            out_specs=[HBM],
            scratch=[dma((2,))],
            aliases={1: 0},
            name="others",
        )[0]
    kept, *parts = call(
        functools.partial(scatter_kernel, shards),
        [part] * shards,
        [VMEM] * 3,
        near,
        middle,
        far,
        scratch=[whole],
        name="scatter",
    )
    return call(
        functools.partial(join_kernel, shards),
        whole_out,
        [VMEM] * shards,
        kept,
        *swapped(parts),
        out_specs=[HBM],
        scratch=[dma((shards,))],
        name="join",
    )[0]


def solution(mesh):
    in_specs = (
        P(("elem", "state"), None, None),
        P(),
        P("elem"),
        P("elem", None),
        P("elem", None, None, None),
    )
    out_specs = P(("elem", "state"), None, None)
    return jax.shard_map(on_device, mesh=mesh, in_specs=in_specs, out_specs=out_specs, check_vma=False)
```

```python
import functools

import jax
import jax.numpy as jnp
from jax import lax
from jax.experimental import pallas as pl
from jax.experimental.pallas import tpu as pltpu
from jax.sharding import PartitionSpec as P

DEG = 4
FULL = 128
LONG = 20 * 10**9

center_shift = 0.2
half_span = 1.1

VMEM = pl.BlockSpec(memory_space=pltpu.VMEM)
HBM = pl.BlockSpec(memory_space=pltpu.HBM)
ANY = pl.BlockSpec(memory_space=pl.ANY)


def call(kernel, outs, ins, *args, out_specs=None, scratch=(), aliases=None, limit=4 << 20, flops=0, name=None):
    return pl.pallas_call(
        kernel,
        out_shape=outs,
        in_specs=ins,
        out_specs=out_specs or [VMEM] * len(outs),
        scratch_shapes=list(scratch),
        input_output_aliases=aliases or {},
        compiler_params=pltpu.CompilerParams(vmem_limit_bytes=limit),
        cost_estimate=pl.CostEstimate(flops=flops, bytes_accessed=1024, transcendentals=0),
        name=name,
    )(*args)


def bf16(*shape):
    return jax.ShapeDtypeStruct(shape, jnp.bfloat16)


def without(body, at, *refs):
    body(*refs[:at], *refs[at + 1 :])


def flipped(shards):
    return lax.axis_index("state") == 1 if shards == 2 else False


def choose(flip, yes, no):
    return no if flip is False else jnp.where(flip, yes, no)


def rows_below(count, rows, lanes):
    return lax.broadcasted_iota(jnp.int32, (rows, lanes), 0) < count


def turn(shards, k, element, weights, count):
    rows, lanes = element.shape[0], weights.shape[1] // shards
    at = lax.rem(lax.axis_index("state") + k, shards) * lanes
    turned = jnp.dot(element, weights[:, pl.ds(pl.multiple_of(at, lanes), lanes)], preferred_element_type=jnp.float32)
    return jnp.where(rows_below(count, rows, lanes), turned, 0.0).astype(jnp.bfloat16)


def fetch_kernel(shards, reach, orbitals, rotation, counts, neighbors, *refs):
    outs, (held, weights, limits, beside, scalars, sems) = refs[:-6], refs[-6:]
    elems = orbitals.shape[0]
    me, flip = lax.axis_index("state"), flipped(shards)
    copies = [
        pltpu.make_async_copy(source, target, sems.at[i])
        for i, (source, target) in enumerate(
            [(rotation, weights), (counts, scalars), (orbitals, held), (counts, limits), (neighbors, beside)]
        )
    ]
    for copy in copies:
        copy.start()
    for copy in copies[:3]:
        copy.wait()
    first = reach if shards == 2 else 0
    for k, out in enumerate(outs):
        for at in range(out.shape[0]):
            e = choose(flip, (first + at + elems - reach) % elems, first + at)
            out[at] = turn(shards, k + 1, held[e], weights, scalars[me * elems + e])
    for copy in copies[3:]:
        copy.wait()


def rotate_kernel(shards, reach, k, held, weights, limits, *outs):
    me, flip = lax.axis_index("state"), flipped(shards)
    elems = held.shape[0]
    ends = limits[...]
    spots = [(out, e) for out in outs for e in range(out.shape[0])]
    for spot, (out, at) in enumerate(spots):
        e = choose(flip, (spot + elems - reach) % elems, spot)
        count = ends[spot]
        for shard in range(shards):
            here = (spot + elems - reach) % elems if shard == 1 and flip is not False else spot
            count = jnp.where(me == shard, ends[shard * elems + here], count)
        out[at] = turn(shards, k, held[e], weights, count)


def table_kernel(total, shards, reach, beside, limits, table):
    couplings, elems = beside.shape
    flip, groups = flipped(shards), elems // reach
    column = lax.broadcasted_iota(jnp.int32, beside.shape, 1)
    offset = beside[...] - (column + lax.axis_index("elem") * elems)
    offset = jnp.where(offset > reach, offset - total, jnp.where(offset < -reach, offset + total, offset))
    place = offset + (column - sum(jnp.where(column >= g * reach, reach, 0) for g in range(1, groups))) + reach
    past = sum(jnp.where(place >= g * reach, reach, 0) for g in range(1, groups))
    place = choose(flip, place + (elems - reach) - 2 * past, place)
    ends = limits[...].reshape(1, elems)

    def mirrored(x):
        parts = [x[:, g * reach : (g + 1) * reach] for g in reversed(range(groups))]
        return choose(flip, jnp.concatenate(parts, axis=1), x)

    table[:couplings] = mirrored(place)
    table[couplings:] = mirrored(ends)


def pack_kernel(shards, group, blocks, packed):
    elems, couplings, _, _ = blocks.shape
    width = packed.shape[0]
    first = choose(flipped(shards), elems - (group + 1) * width, group * width)
    for e in range(width):
        for k in range(couplings):
            packed[e, :, k * FULL : (k + 1) * FULL] = blocks[first + e, k, :, :FULL]
        tail = [blocks[first + e, k, :, FULL:] for k in range(couplings)]
        packed[e, :, couplings * FULL :] = jnp.concatenate(tail, axis=1)


def middle_kernel(half, arrived, leaving, middle, copied):
    flip, share = flipped(2), half.shape[0]
    copied[...] = leaving[...]
    middle[pl.ds(choose(flip, share, 0), share)] = half[...]
    middle[pl.ds(choose(flip, 0, share), share)] = arrived[...]


def gather_kernel(shards, *refs):
    me = lax.axis_index("state")
    parts, groups, whole = refs[:shards], refs[shards : shards + 3], refs[-1]
    elems, width = parts[0].shape[0], groups[0].shape[0]
    for k, part in enumerate(parts):
        whole[pl.ds(lax.rem(me + shards - k, shards) * elems, elems)] = part[...]
    for g, group in enumerate(groups):
        group[...] = whole[g * width : (g + 1) * width]


def level_kernel(first, factor, with_prev, packed, table, before, here, after, *refs):
    refs, window = list(refs[:-1]), refs[-1]
    previous = refs.pop(0) if with_prev else None
    out = refs[0]
    width, rows, lanes = here.shape
    for g, group in enumerate((before, here, after)):
        window[g * width : (g + 1) * width] = group[...]
    places = table[...]
    couplings = places.shape[0] - 1
    for e in range(width):
        at = [places[k, first + e] for k in range(couplings)]
        fields = [window[i, :FULL] for i in at] + [window[i, FULL:] for i in at]
        image = jnp.dot(packed[e], jnp.concatenate(fields, axis=0), preferred_element_type=jnp.float32)
        image = jnp.where(rows_below(places[couplings, first + e], rows, lanes), image, 0.0)
        value = factor * (image - center_shift * here[e].astype(jnp.float32)) / half_span
        if with_prev:
            value = value - previous[e].astype(jnp.float32)
        out[e] = value.astype(jnp.bfloat16)
    if len(refs) > 1:
        share = refs[1].shape[0]
        refs[1][...] = out[pl.ds(choose(flipped(2), 0, width - share), share)]


def scatter_kernel(shards, *refs):
    me = lax.axis_index("state")
    groups, parts, whole = refs[:3], refs[3:-1], refs[-1]
    elems, width = parts[0].shape[0], groups[0].shape[0]
    for g, group in enumerate(groups):
        whole[g * width : (g + 1) * width] = group[...]
    for k, part in enumerate(parts):
        part[...] = whole[pl.ds(lax.rem(me + k, shards) * elems, elems)]


def place(shards, k, first, part, out, sem):
    elems, _, lanes = part.shape
    at = lax.rem(lax.axis_index("state") + shards - k, shards) * lanes
    return pltpu.make_async_copy(part, out.at[pl.ds(first, elems), :, pl.ds(pl.multiple_of(at, lanes), lanes)], sem)


def run(copies):
    for copy in copies:
        copy.start()
    for copy in copies:
        copy.wait()


def near_copy(k, near, out, sem):
    return place(2, k, choose(flipped(2), out.shape[0] - near.shape[0], 0), near, out, sem)


def half_copy(k, half, out, sem):
    return place(2, k, choose(flipped(2), 0, out.shape[0] - half.shape[0]), half, out, sem)


def own_kernel(near, middle, half, out, sems):
    share = half.shape[0]
    kept = middle.at[pl.ds(choose(flipped(2), share, 0), share)]
    run([near_copy(0, near, out, sems.at[0]), half_copy(0, kept, out, sems.at[1]), half_copy(1, half, out, sems.at[2])])


def others_kernel(far, out, sem):
    run([near_copy(1, far, out, sem)])


def join_kernel(shards, *refs):
    parts, out, sems = refs[:shards], refs[-2], refs[-1]
    run([place(shards, k, 0, part, out, sems.at[k]) for k, part in enumerate(parts)])


def on_device(orbitals, rotation, counts, neighbors, blocks):
    row_elems, rows, states = orbitals.shape
    elems, couplings = neighbors.shape
    inputs = [
        pltpu.with_memory_space_constraint(x, pltpu.HBM) for x in (orbitals, rotation, counts, neighbors.T)
    ]
    shards = lax.axis_size("state")
    ring = lax.axis_size("elem")
    width = elems // 3
    lanes = states // shards
    group, part = bf16(width, rows, lanes), bf16(row_elems, rows, lanes)
    half = bf16(row_elems - width, rows, lanes)
    whole = pltpu.VMEM((elems, rows, lanes), jnp.bfloat16)
    scalars = pltpu.SMEM(counts.shape, jnp.int32)
    dma = pltpu.SemaphoreType.DMA
    pair = shards == 2

    def shifted(x, step, across=False):
        moves = []
        for i in range(ring):
            for j in range(shards):
                to = (i + (-step if pair and j == 1 else step)) % ring
                moves.append((i * shards + j, to * shards + (1 - j if across else j)))
        return lax.ppermute(x, ("elem", "state"), moves)

    def to_far_of_neighbor(x):
        return shifted(x, -1)

    def to_near_of_neighbor(x):
        return shifted(x, 1)

    def swapped(parts):
        return [
            lax.ppermute(x, "state", [(i, (i + k + 1) % shards) for i in range(shards)]) for k, x in enumerate(parts)
        ]

    *parts, held, weights, limits, beside = call(
        functools.partial(fetch_kernel, shards, width),
        ([half] if pair else [part] * (shards - 1)) + [jax.ShapeDtypeStruct(x.shape, x.dtype) for x in inputs],
        [HBM] * len(inputs),
        *inputs,
        scratch=[scalars, dma((5,))],
        flops=LONG,
        name="fetch",
    )
    if pair:
        arrived_half = swapped(parts)[0]
        leaving = call(
            functools.partial(rotate_kernel, shards, width, 1), [group], [VMEM] * 3, held, weights, limits, name="rotate_out"
        )[0]
        near_halo = shifted(leaving, -1, across=True)
        kept = call(
            functools.partial(without, functools.partial(rotate_kernel, shards, width, 0), 3),
            [group, half],
            [VMEM] * 3 + [ANY],
            held,
            weights,
            limits,
            leaving,
            name="rotate_in",
        )
        far_halo = to_far_of_neighbor(kept[0])
    else:
        arrived = swapped(parts)
        kept = call(
            functools.partial(rotate_kernel, shards, width, 0), [part], [VMEM] * 3, held, weights, limits, name="rotate_in"
        )
    table = call(
        functools.partial(without, functools.partial(table_kernel, elems * ring, shards, width), 2),
        [jax.ShapeDtypeStruct((couplings + 1, elems), jnp.int32)],
        [VMEM, VMEM, ANY],
        beside,
        limits,
        kept[0],
        name="table",
    )[0]

    def pack(g, behind):
        return call(
            functools.partial(without, functools.partial(pack_kernel, shards, g), 1),
            [bf16(width, rows, couplings * rows)],
            [VMEM, ANY],
            blocks,
            behind,
            name="pack",
        )[0]

    packed = {0: pack(0, table)}
    packed[2] = pack(2, packed[0])
    packed[1] = pack(1, packed[2])
    if pair:
        near = kept[0]
        middle, leaving = call(
            functools.partial(without, middle_kernel, 3),
            [group] * 2,
            [VMEM] * 3 + [ANY],
            kept[1],
            arrived_half,
            leaving,
            packed[1],
            name="gather",
        )
        far = swapped([leaving])[0]
    else:
        near, middle, far = call(
            functools.partial(without, functools.partial(gather_kernel, shards), shards),
            [group] * 3,
            [VMEM] * shards + [ANY],
            *kept,
            *arrived,
            packed[1],
            scratch=[whole],
            name="gather",
        )
        near_halo, far_halo = to_near_of_neighbor(far), to_far_of_neighbor(near)

    def level(g, m, before, here, after, previous, split=False, behind=None, flops=0):
        body = functools.partial(level_kernel, g * width, 1.0 if m == 1 else 2.0, previous is not None)
        args = [packed[g], table, before, here, after] + ([] if previous is None else [previous])
        specs = [VMEM] * len(args)
        if behind is not None:
            body = functools.partial(without, body, len(args))
            args, specs = args + [behind], specs + [ANY]
        outs = call(
            body,
            [group] + [half] * split,
            specs,
            *args,
            scratch=[pltpu.VMEM((3 * width, rows, lanes), jnp.bfloat16)],
            flops=flops,
            name=("near", "middle", "far")[g] + str(m),
        )
        return outs if split else outs[0]

    older = (None, None, None)
    for m in range(1, DEG + 1):
        last = m == DEG
        behind = half_arrived = None
        if m > 2:
            new_middle = behind = level(1, m, near, middle, far, older[1], split=pair and last)
            if pair and last:
                new_middle, half_leaving = new_middle
                behind, half_arrived = None, swapped([half_leaving])[0]
        if m % 2:
            new_near = level(0, m, near_halo, near, middle, older[0], behind=behind)
            next_far_halo = to_far_of_neighbor(new_near)
            new_far = level(2, m, middle, far, far_halo, older[2], behind=new_near)
            next_near_halo = to_near_of_neighbor(new_far)
        else:
            new_far = level(2, m, middle, far, far_halo, older[2], behind=behind)
            if m == 2:
                new_middle = level(1, m, near, middle, far, older[1], behind=new_far)
            if last and pair:
                arrived = swapped([new_far])[0]
            else:
                next_near_halo = to_near_of_neighbor(new_far)
            behind = half_arrived if last else new_middle
            new_near = level(0, m, near_halo, near, middle, older[0], behind=behind, flops=LONG * last)
            if not last:
                next_far_halo = to_far_of_neighbor(new_near)
        if m == 1:
            new_middle = level(1, m, near, middle, far, older[1])
        if not last:
            near_halo, far_halo = next_near_halo, next_far_halo
        older, (near, middle, far) = (near, middle, far), (new_near, new_middle, new_far)

    whole_out = [bf16(*orbitals.shape)]
    if pair:
        out = call(
            own_kernel,
            whole_out,
            [VMEM] * 3,
            near,
            middle,
            half_arrived,
            out_specs=[HBM],
            scratch=[dma((3,))],
            name="own",
        )[0]
        return call(
            functools.partial(without, others_kernel, 1),
            whole_out,
            [VMEM, HBM],
            arrived,
            out,
            out_specs=[HBM],
            scratch=[dma],
            aliases={1: 0},
            name="others",
        )[0]
    kept, *parts = call(
        functools.partial(scatter_kernel, shards),
        [part] * shards,
        [VMEM] * 3,
        near,
        middle,
        far,
        scratch=[whole],
        name="scatter",
    )
    return call(
        functools.partial(join_kernel, shards),
        whole_out,
        [VMEM] * shards,
        kept,
        *swapped(parts),
        out_specs=[HBM],
        scratch=[dma((shards,))],
        name="join",
    )[0]


def solution(mesh):
    in_specs = (
        P(("elem", "state"), None, None),
        P(),
        P("elem"),
        P("elem", None),
        P("elem", None, None, None),
    )
    out_specs = P(("elem", "state"), None, None)
    return jax.shard_map(on_device, mesh=mesh, in_specs=in_specs, out_specs=out_specs, check_vma=False)
```

```python
import functools

import jax
import jax.numpy as jnp
from jax import lax
from jax.experimental import pallas as pl
from jax.experimental.pallas import tpu as pltpu
from jax.sharding import PartitionSpec as P

DEG = 4
FULL = 128
LONG = 20 * 10**9

center_shift = 0.2
half_span = 1.1

VMEM = pl.BlockSpec(memory_space=pltpu.VMEM)
HBM = pl.BlockSpec(memory_space=pltpu.HBM)
ANY = pl.BlockSpec(memory_space=pl.ANY)


def call(kernel, outs, ins, *args, out_specs=None, scratch=(), aliases=None, limit=4 << 20, flops=0, name=None):
    return pl.pallas_call(
        kernel,
        out_shape=outs,
        in_specs=ins,
        out_specs=out_specs or [VMEM] * len(outs),
        scratch_shapes=list(scratch),
        input_output_aliases=aliases or {},
        compiler_params=pltpu.CompilerParams(vmem_limit_bytes=limit),
        cost_estimate=pl.CostEstimate(flops=flops, bytes_accessed=1024, transcendentals=0),
        name=name,
    )(*args)


def bf16(*shape):
    return jax.ShapeDtypeStruct(shape, jnp.bfloat16)


def without(body, at, count, *refs):
    body(*refs[:at], *refs[at + count :])


def flipped(shards):
    return lax.axis_index("state") == 1 if shards == 2 else False


def choose(flip, yes, no):
    return no if flip is False else jnp.where(flip, yes, no)


def rows_below(count, rows, lanes):
    return lax.broadcasted_iota(jnp.int32, (rows, lanes), 0) < count


def turn(shards, k, element, weights, count):
    rows, lanes = element.shape[0], weights.shape[1] // shards
    at = lax.rem(lax.axis_index("state") + k, shards) * lanes
    turned = jnp.dot(element, weights[:, pl.ds(pl.multiple_of(at, lanes), lanes)], preferred_element_type=jnp.float32)
    return jnp.where(rows_below(count, rows, lanes), turned, 0.0).astype(jnp.bfloat16)


def rotate_kernel(shards, reach, k, first, held, weights, limits, *outs):
    me, flip = lax.axis_index("state"), flipped(shards)
    elems = held.shape[0]
    ends = limits[...]
    spots = [(out, e) for out in outs for e in range(out.shape[0])]
    for spot, (out, at) in enumerate(spots, first):
        e = choose(flip, (spot + elems - reach) % elems, spot)
        count = ends[spot]
        for shard in range(shards):
            here = (spot + elems - reach) % elems if shard == 1 and flip is not False else spot
            count = jnp.where(me == shard, ends[shard * elems + here], count)
        out[at] = turn(shards, k, held[e], weights, count)


def fetch_kernel(shards, reach, orbitals, rotation, counts, neighbors, *refs):
    outs, (held, weights, limits, beside, sems) = refs[:-5], refs[-5:]
    copies = [
        pltpu.make_async_copy(source, target, sems.at[i])
        for i, (source, target) in enumerate(
            [(rotation, weights), (counts, limits), (orbitals, held), (neighbors, beside)]
        )
    ]
    for copy in copies:
        copy.start()
    for copy in copies[:3]:
        copy.wait()
    for k, out in enumerate(outs):
        rotate_kernel(shards, reach, k + 1, reach if shards == 2 else 0, held, weights, limits, out)
    copies[3].wait()


def table_kernel(total, shards, reach, beside, limits, table):
    couplings, elems = beside.shape
    flip, groups = flipped(shards), elems // reach
    column = lax.broadcasted_iota(jnp.int32, beside.shape, 1)
    offset = beside[...] - (column + lax.axis_index("elem") * elems)
    offset = jnp.where(offset > reach, offset - total, jnp.where(offset < -reach, offset + total, offset))
    place = offset + (column - sum(jnp.where(column >= g * reach, reach, 0) for g in range(1, groups))) + reach
    past = sum(jnp.where(place >= g * reach, reach, 0) for g in range(1, groups))
    place = choose(flip, place + (elems - reach) - 2 * past, place)
    ends = limits[...].reshape(1, elems)

    def mirrored(x):
        parts = [x[:, g * reach : (g + 1) * reach] for g in reversed(range(groups))]
        return choose(flip, jnp.concatenate(parts, axis=1), x)

    rows = jnp.concatenate([mirrored(place), mirrored(ends)], axis=0)
    for e in range(elems):
        for k in range(couplings + 1):
            table[e, k] = jnp.full(table.shape[2:], rows[k, e], jnp.int32)


def pack_kernel(shards, group, blocks, packed):
    elems, couplings, _, _ = blocks.shape
    width = packed.shape[0]
    first = choose(flipped(shards), elems - (group + 1) * width, group * width)
    for e in range(width):
        for k in range(couplings):
            packed[e, :, k * FULL : (k + 1) * FULL] = blocks[first + e, k, :, :FULL]
        tail = [blocks[first + e, k, :, FULL:] for k in range(couplings)]
        packed[e, :, couplings * FULL :] = jnp.concatenate(tail, axis=1)


def middle_kernel(half, arrived, leaving, middle, copied):
    flip, share = flipped(2), half.shape[0]
    copied[...] = leaving[...]
    middle[pl.ds(choose(flip, share, 0), share)] = half[...]
    middle[pl.ds(choose(flip, 0, share), share)] = arrived[...]


def gather_kernel(shards, *refs):
    me = lax.axis_index("state")
    parts, groups, whole = refs[:shards], refs[shards : shards + 3], refs[-1]
    elems, width = parts[0].shape[0], groups[0].shape[0]
    for k, part in enumerate(parts):
        whole[pl.ds(lax.rem(me + shards - k, shards) * elems, elems)] = part[...]
    for g, group in enumerate(groups):
        group[...] = whole[g * width : (g + 1) * width]


def hard():
    return lax.rem(lax.axis_index("elem") + lax.axis_index("state"), 2)


def level_if_kernel(which, instead, body, at, *refs):
    if instead:
        other, refs = refs[at], refs[:at] + refs[at + 1 :]

        @pl.when(hard() != which)
        def _():
            refs[-2][...] = other[...]

    pl.when(hard() == which)(functools.partial(body, *refs))


def level_kernel(first, factor, with_prev, packed, table, before, here, after, *refs):
    refs, window = list(refs[:-1]), refs[-1]
    previous = refs.pop(0) if with_prev else None
    out = refs[0]
    width, rows, lanes = here.shape
    for g, group in enumerate((before, here, after)):
        window[g * width : (g + 1) * width] = group[...]
    couplings = table.shape[1] - 1
    for e in range(width):
        *at, end = [table[first + e, k, 0, 0] for k in range(couplings + 1)]
        fields = [window[i, :FULL] for i in at] + [window[i, FULL:] for i in at]
        image = jnp.dot(packed[e], jnp.concatenate(fields, axis=0), preferred_element_type=jnp.float32)
        image = jnp.where(rows_below(end, rows, lanes), image, 0.0)
        value = factor * (image - center_shift * here[e].astype(jnp.float32)) / half_span
        if with_prev:
            value = value - previous[e].astype(jnp.float32)
        out[e] = value.astype(jnp.bfloat16)
    if len(refs) > 1:
        share = refs[1].shape[0]
        refs[1][...] = out[pl.ds(choose(flipped(2), 0, width - share), share)]


def scatter_kernel(shards, *refs):
    me = lax.axis_index("state")
    groups, parts, whole = refs[:3], refs[3:-1], refs[-1]
    elems, width = parts[0].shape[0], groups[0].shape[0]
    for g, group in enumerate(groups):
        whole[g * width : (g + 1) * width] = group[...]
    for k, part in enumerate(parts):
        part[...] = whole[pl.ds(lax.rem(me + k, shards) * elems, elems)]


def place(shards, k, first, part, out, sem):
    elems, _, lanes = part.shape
    at = lax.rem(lax.axis_index("state") + shards - k, shards) * lanes
    return pltpu.make_async_copy(part, out.at[pl.ds(first, elems), :, pl.ds(pl.multiple_of(at, lanes), lanes)], sem)


def run(copies):
    for copy in copies:
        copy.start()
    for copy in copies:
        copy.wait()


def near_copy(k, near, out, sem):
    return place(2, k, choose(flipped(2), out.shape[0] - near.shape[0], 0), near, out, sem)


def half_copy(k, half, out, sem):
    return place(2, k, choose(flipped(2), 0, out.shape[0] - half.shape[0]), half, out, sem)


def own_kernel(near, middle, half, out, sems):
    share = half.shape[0]
    kept = middle.at[pl.ds(choose(flipped(2), share, 0), share)]
    run([near_copy(0, near, out, sems.at[0]), half_copy(0, kept, out, sems.at[1]), half_copy(1, half, out, sems.at[2])])


def others_kernel(far, out, sem):
    run([near_copy(1, far, out, sem)])


def join_kernel(shards, *refs):
    parts, out, sems = refs[:shards], refs[-2], refs[-1]
    run([place(shards, k, 0, part, out, sems.at[k]) for k, part in enumerate(parts)])


def on_device(orbitals, rotation, counts, neighbors, blocks):
    row_elems, rows, states = orbitals.shape
    elems, couplings = neighbors.shape
    inputs = [
        pltpu.with_memory_space_constraint(x, pltpu.HBM) for x in (orbitals, rotation, counts, neighbors.T)
    ]
    shards = lax.axis_size("state")
    ring = lax.axis_size("elem")
    width = elems // 3
    lanes = states // shards
    group, part = bf16(width, rows, lanes), bf16(row_elems, rows, lanes)
    half = bf16(row_elems - width, rows, lanes)
    whole = pltpu.VMEM((elems, rows, lanes), jnp.bfloat16)
    dma = pltpu.SemaphoreType.DMA
    pair = shards == 2

    def permuted(x, target):
        moves = []
        for i in range(ring):
            for j in range(shards):
                to_i, to_j = target(i, j)
                moves.append((i * shards + j, to_i % ring * shards + to_j))
        return lax.ppermute(x, ("elem", "state"), moves)

    def shifted(x, step, across=False):
        return permuted(x, lambda i, j: (i + (-step if pair and j == 1 else step), 1 - j if across else j))

    def to_far_of_neighbor(x):
        return shifted(x, -1)

    def to_near_of_neighbor(x):
        return shifted(x, 1)

    def swapped(parts):
        return [
            lax.ppermute(x, "state", [(i, (i + k + 1) % shards) for i in range(shards)]) for k, x in enumerate(parts)
        ]

    *parts, held, weights, limits, beside = call(
        functools.partial(fetch_kernel, shards, width),
        ([half] if pair else [part] * (shards - 1)) + [jax.ShapeDtypeStruct(x.shape, x.dtype) for x in inputs],
        [HBM] * len(inputs),
        *inputs,
        scratch=[dma((4,))],
        name="fetch",
    )
    if pair:
        arrived_half = swapped(parts)[0]
        leaving = call(
            functools.partial(rotate_kernel, shards, width, 1, 0), [group], [VMEM] * 3, held, weights, limits, flops=LONG, name="rotate_out"
        )[0]
        near_halo = shifted(leaving, -1, across=True)
        kept = call(
            functools.partial(without, functools.partial(rotate_kernel, shards, width, 0, 0), 3, 1),
            [group, half],
            [VMEM] * 3 + [ANY],
            held,
            weights,
            limits,
            leaving,
            name="rotate_in",
        )
        far_halo = to_far_of_neighbor(kept[0])
    else:
        arrived = swapped(parts)
        kept = call(
            functools.partial(rotate_kernel, shards, width, 0, 0), [part], [VMEM] * 3, held, weights, limits, name="rotate_in"
        )
    table = call(
        functools.partial(without, functools.partial(table_kernel, elems * ring, shards, width), 2, 1),
        [jax.ShapeDtypeStruct((elems, couplings + 1, 8, 128), jnp.int32)],
        [VMEM, VMEM, ANY],
        beside,
        limits,
        kept[0],
        name="table",
    )[0]

    def pack(g, behind):
        return call(
            functools.partial(without, functools.partial(pack_kernel, shards, g), 1, 1),
            [bf16(width, rows, couplings * rows)],
            [VMEM, ANY],
            blocks,
            behind,
            name="pack",
        )[0]

    packed = {0: pack(0, table)}
    packed[2] = pack(2, packed[0])
    packed[1] = pack(1, packed[2])
    if pair:
        near = kept[0]
        middle, leaving = call(
            functools.partial(without, middle_kernel, 3, 1),
            [group] * 2,
            [VMEM] * 3 + [ANY],
            kept[1],
            arrived_half,
            leaving,
            packed[1],
            name="gather",
        )
        far = swapped([leaving])[0]
    else:
        near, middle, far = call(
            functools.partial(without, functools.partial(gather_kernel, shards), shards, 1),
            [group] * 3,
            [VMEM] * shards + [ANY],
            *kept,
            *arrived,
            packed[1],
            scratch=[whole],
            name="gather",
        )
        near_halo, far_halo = to_near_of_neighbor(far), to_far_of_neighbor(near)

    def level(g, m, before, here, after, previous, which=None, instead=None, split=False, behind=(), flops=0):
        body = functools.partial(level_kernel, g * width, 1.0 if m == 1 else 2.0, previous is not None)
        args = [packed[g], table, before, here, after] + ([] if previous is None else [previous])
        if which is not None:
            body = functools.partial(level_if_kernel, which, instead is not None, body, len(args))
            args += [] if instead is None else [instead]
        specs = [VMEM] * len(args)
        if behind:
            body = functools.partial(without, body, len(args), len(behind))
            args, specs = args + list(behind), specs + [ANY] * len(behind)
        outs = call(
            body,
            [group] + [half] * split,
            specs,
            *args,
            scratch=[pltpu.VMEM((3 * width, rows, lanes), jnp.bfloat16)],
            flops=flops,
            name=("near", "middle", "far")[g] + str(m),
        )
        return outs if split else outs[0]

    older = (None, None, None)
    for m in range(1, DEG + 1):
        last = m == DEG
        if m == 1:
            new_near = level(0, m, near_halo, near, middle, older[0])
            next_far_halo = to_far_of_neighbor(new_near)
            new_far = level(2, m, middle, far, far_halo, older[2], behind=[new_near])
            next_near_halo = to_near_of_neighbor(new_far)
            new_middle = level(1, m, near, middle, far, older[1])
        elif m % 2:
            new_middle = level(1, m, near, middle, far, older[1])
            new_near = level(0, m, near_halo, near, middle, older[0], behind=[new_middle])
            next_far_halo = to_far_of_neighbor(new_near)
            new_far = level(2, m, middle, far, far_halo, older[2], behind=[new_near])
            next_near_halo = to_near_of_neighbor(new_far)
        elif not last:
            new_far = level(2, m, middle, far, far_halo, older[2])
            next_near_halo = to_near_of_neighbor(new_far)
            new_middle = level(1, m, near, middle, far, older[1], behind=[new_far])
            new_near = level(0, m, near_halo, near, middle, older[0], behind=[new_middle])
            next_far_halo = to_far_of_neighbor(new_near)
        else:
            if pair:
                mate_halo = permuted(near, lambda i, j: (i ^ 1, j))
                early = level(2, m, middle, far, mate_halo, older[2], which=0)
                new_middle, half_leaving = level(1, m, near, middle, far, older[1], split=True, behind=[early])
                half_arrived = swapped([half_leaving])[0]
                new_far = level(2, m, middle, far, far_halo, older[2], which=1, instead=early)
                arrived = swapped([new_far])[0]
            else:
                new_middle = level(1, m, near, middle, far, older[1])
                new_far = level(2, m, middle, far, far_halo, older[2])
            behind = [half_arrived] if pair else []
            new_near = level(0, m, near_halo, near, middle, older[0], behind=behind, flops=LONG)
        if not last:
            near_halo, far_halo = next_near_halo, next_far_halo
        older, (near, middle, far) = (near, middle, far), (new_near, new_middle, new_far)

    whole_out = [bf16(*orbitals.shape)]
    if pair:
        out = call(
            own_kernel,
            whole_out,
            [VMEM] * 3,
            near,
            middle,
            half_arrived,
            out_specs=[HBM],
            scratch=[dma((3,))],
            name="own",
        )[0]
        return call(
            functools.partial(without, others_kernel, 1, 1),
            whole_out,
            [VMEM, HBM],
            arrived,
            out,
            out_specs=[HBM],
            scratch=[dma],
            aliases={1: 0},
            name="others",
        )[0]
    kept, *parts = call(
        functools.partial(scatter_kernel, shards),
        [part] * shards,
        [VMEM] * 3,
        near,
        middle,
        far,
        scratch=[whole],
        name="scatter",
    )
    return call(
        functools.partial(join_kernel, shards),
        whole_out,
        [VMEM] * shards,
        kept,
        *swapped(parts),
        out_specs=[HBM],
        scratch=[dma((shards,))],
        name="join",
    )[0]


def solution(mesh):
    in_specs = (
        P(("elem", "state"), None, None),
        P(),
        P("elem"),
        P("elem", None),
        P("elem", None, None, None),
    )
    out_specs = P(("elem", "state"), None, None)
    return jax.shard_map(on_device, mesh=mesh, in_specs=in_specs, out_specs=out_specs, check_vma=False)
```

```python
import functools

import jax
import jax.numpy as jnp
from jax import lax
from jax.experimental import pallas as pl
from jax.experimental.pallas import tpu as pltpu
from jax.sharding import PartitionSpec as P

DEG = 4
FULL = 128
LONG, SHORT = 20 * 10**9, 10**9

center_shift = 0.2
half_span = 1.1

VMEM = pl.BlockSpec(memory_space=pltpu.VMEM)
HBM = pl.BlockSpec(memory_space=pltpu.HBM)
ANY = pl.BlockSpec(memory_space=pl.ANY)


def call(kernel, outs, ins, *args, out_specs=None, scratch=(), aliases=None, limit=4 << 20, flops=0, name=None):
    return pl.pallas_call(
        kernel,
        out_shape=outs,
        in_specs=ins,
        out_specs=out_specs or [VMEM] * len(outs),
        scratch_shapes=list(scratch),
        input_output_aliases=aliases or {},
        compiler_params=pltpu.CompilerParams(vmem_limit_bytes=limit),
        cost_estimate=pl.CostEstimate(flops=flops, bytes_accessed=1024, transcendentals=0),
        name=name,
    )(*args)


def bf16(*shape):
    return jax.ShapeDtypeStruct(shape, jnp.bfloat16)


def without(body, at, count, *refs):
    body(*refs[:at], *refs[at + count :])


def flipped(shards):
    return lax.axis_index("state") == 1 if shards == 2 else False


def choose(flip, yes, no):
    return no if flip is False else jnp.where(flip, yes, no)


def rows_below(count, rows, lanes):
    return lax.broadcasted_iota(jnp.int32, (rows, lanes), 0) < count


def turn(shards, k, element, weights, count):
    rows, lanes = element.shape[0], weights.shape[1] // shards
    at = lax.rem(lax.axis_index("state") + k, shards) * lanes
    turned = jnp.dot(element, weights[:, pl.ds(pl.multiple_of(at, lanes), lanes)], preferred_element_type=jnp.float32)
    return jnp.where(rows_below(count, rows, lanes), turned, 0.0).astype(jnp.bfloat16)


def rotate_kernel(shards, reach, k, first, held, weights, limits, *outs):
    me, flip = lax.axis_index("state"), flipped(shards)
    elems = held.shape[0]
    ends = limits[...]
    spots = [(out, e) for out in outs for e in range(out.shape[0])]
    for spot, (out, at) in enumerate(spots, first):
        e = choose(flip, (spot + elems - reach) % elems, spot)
        count = ends[spot]
        for shard in range(shards):
            here = (spot + elems - reach) % elems if shard == 1 and flip is not False else spot
            count = jnp.where(me == shard, ends[shard * elems + here], count)
        out[at] = turn(shards, k, held[e], weights, count)


def fetch_kernel(shards, reach, orbitals, rotation, counts, neighbors, *refs):
    outs, (held, weights, limits, beside, sems) = refs[:-5], refs[-5:]
    copies = [
        pltpu.make_async_copy(source, target, sems.at[i])
        for i, (source, target) in enumerate(
            [(rotation, weights), (counts, limits), (orbitals, held), (neighbors, beside)]
        )
    ]
    for copy in copies:
        copy.start()
    for copy in copies[:3]:
        copy.wait()
    if shards == 2:
        near, half = outs
        rotate_kernel(shards, reach, 1, reach, held, weights, limits, half)
        rotate_kernel(shards, reach, 1, 0, held, weights, limits, near)
    else:
        for k, out in enumerate(outs):
            rotate_kernel(shards, reach, k + 1, 0, held, weights, limits, out)
    copies[3].wait()


def table_kernel(total, shards, reach, beside, limits, table):
    couplings, elems = beside.shape
    flip, groups = flipped(shards), elems // reach
    column = lax.broadcasted_iota(jnp.int32, beside.shape, 1)
    offset = beside[...] - (column + lax.axis_index("elem") * elems)
    offset = jnp.where(offset > reach, offset - total, jnp.where(offset < -reach, offset + total, offset))
    place = offset + (column - sum(jnp.where(column >= g * reach, reach, 0) for g in range(1, groups))) + reach
    past = sum(jnp.where(place >= g * reach, reach, 0) for g in range(1, groups))
    place = choose(flip, place + (elems - reach) - 2 * past, place)
    ends = limits[...].reshape(1, elems)

    def mirrored(x):
        parts = [x[:, g * reach : (g + 1) * reach] for g in reversed(range(groups))]
        return choose(flip, jnp.concatenate(parts, axis=1), x)

    rows = jnp.concatenate([mirrored(place), mirrored(ends)], axis=0)
    for e in range(elems):
        for k in range(couplings + 1):
            table[e, k] = jnp.full(table.shape[2:], rows[k, e], jnp.int32)


def pack_kernel(shards, group, blocks, packed):
    elems, couplings, _, _ = blocks.shape
    width = packed.shape[0]
    first = choose(flipped(shards), elems - (group + 1) * width, group * width)
    for e in range(width):
        for k in range(couplings):
            packed[e, :, k * FULL : (k + 1) * FULL] = blocks[first + e, k, :, :FULL]
        tail = [blocks[first + e, k, :, FULL:] for k in range(couplings)]
        packed[e, :, couplings * FULL :] = jnp.concatenate(tail, axis=1)


def middle_kernel(half, arrived, leaving, middle, copied):
    flip, share = flipped(2), half.shape[0]
    copied[...] = leaving[...]
    middle[pl.ds(choose(flip, share, 0), share)] = half[...]
    middle[pl.ds(choose(flip, 0, share), share)] = arrived[...]


def gather_kernel(shards, *refs):
    me = lax.axis_index("state")
    parts, groups, whole = refs[:shards], refs[shards : shards + 3], refs[-1]
    elems, width = parts[0].shape[0], groups[0].shape[0]
    for k, part in enumerate(parts):
        whole[pl.ds(lax.rem(me + shards - k, shards) * elems, elems)] = part[...]
    for g, group in enumerate(groups):
        group[...] = whole[g * width : (g + 1) * width]


def hard():
    return lax.rem(lax.axis_index("elem") + lax.axis_index("state"), 2)


def level_if_kernel(which, instead, body, at, *refs):
    if instead:
        other, refs = refs[at], refs[:at] + refs[at + 1 :]

        @pl.when(hard() != which)
        def _():
            refs[-2][...] = other[...]

    pl.when(hard() == which)(functools.partial(body, *refs))


def level_kernel(first, factor, with_prev, packed, table, before, here, after, *refs):
    refs, window = list(refs[:-1]), refs[-1]
    previous = refs.pop(0) if with_prev else None
    out = refs[0]
    width, rows, lanes = here.shape
    for g, group in enumerate((before, here, after)):
        window[g * width : (g + 1) * width] = group[...]
    couplings = table.shape[1] - 1
    for e in range(width):
        *at, end = [table[first + e, k, 0, 0] for k in range(couplings + 1)]
        fields = [window[i, :FULL] for i in at] + [window[i, FULL:] for i in at]
        image = jnp.dot(packed[e], jnp.concatenate(fields, axis=0), preferred_element_type=jnp.float32)
        image = jnp.where(rows_below(end, rows, lanes), image, 0.0)
        value = factor * (image - center_shift * here[e].astype(jnp.float32)) / half_span
        if with_prev:
            value = value - previous[e].astype(jnp.float32)
        out[e] = value.astype(jnp.bfloat16)
    if len(refs) > 1:
        share = refs[1].shape[0]
        refs[1][...] = out[pl.ds(choose(flipped(2), 0, width - share), share)]


def scatter_kernel(shards, *refs):
    me = lax.axis_index("state")
    groups, parts, whole = refs[:3], refs[3:-1], refs[-1]
    elems, width = parts[0].shape[0], groups[0].shape[0]
    for g, group in enumerate(groups):
        whole[g * width : (g + 1) * width] = group[...]
    for k, part in enumerate(parts):
        part[...] = whole[pl.ds(lax.rem(me + k, shards) * elems, elems)]


def place(shards, k, first, part, out, sem):
    elems, _, lanes = part.shape
    at = lax.rem(lax.axis_index("state") + shards - k, shards) * lanes
    return pltpu.make_async_copy(part, out.at[pl.ds(first, elems), :, pl.ds(pl.multiple_of(at, lanes), lanes)], sem)


def run(copies):
    for copy in copies:
        copy.start()
    for copy in copies:
        copy.wait()


def near_copy(k, near, out, sem):
    return place(2, k, choose(flipped(2), out.shape[0] - near.shape[0], 0), near, out, sem)


def half_copy(k, half, out, sem):
    return place(2, k, choose(flipped(2), 0, out.shape[0] - half.shape[0]), half, out, sem)


def own_kernel(near, middle, half, out, sems):
    share = half.shape[0]
    kept = middle.at[pl.ds(choose(flipped(2), share, 0), share)]
    run([near_copy(0, near, out, sems.at[0]), half_copy(0, kept, out, sems.at[1]), half_copy(1, half, out, sems.at[2])])


def others_kernel(far, out, sem):
    run([near_copy(1, far, out, sem)])


def join_kernel(shards, *refs):
    parts, out, sems = refs[:shards], refs[-2], refs[-1]
    run([place(shards, k, 0, part, out, sems.at[k]) for k, part in enumerate(parts)])


def on_device(orbitals, rotation, counts, neighbors, blocks):
    row_elems, rows, states = orbitals.shape
    elems, couplings = neighbors.shape
    inputs = [
        pltpu.with_memory_space_constraint(x, pltpu.HBM) for x in (orbitals, rotation, counts, neighbors.T)
    ]
    shards = lax.axis_size("state")
    ring = lax.axis_size("elem")
    width = elems // 3
    lanes = states // shards
    group, part = bf16(width, rows, lanes), bf16(row_elems, rows, lanes)
    half = bf16(row_elems - width, rows, lanes)
    whole = pltpu.VMEM((elems, rows, lanes), jnp.bfloat16)
    dma = pltpu.SemaphoreType.DMA
    pair = shards == 2

    def permuted(x, target):
        moves = []
        for i in range(ring):
            for j in range(shards):
                to_i, to_j = target(i, j)
                moves.append((i * shards + j, to_i % ring * shards + to_j))
        return lax.ppermute(x, ("elem", "state"), moves)

    def shifted(x, step, across=False):
        return permuted(x, lambda i, j: (i + (-step if pair and j == 1 else step), 1 - j if across else j))

    def to_far_of_neighbor(x):
        return shifted(x, -1)

    def to_near_of_neighbor(x):
        return shifted(x, 1)

    def swapped(parts):
        return [
            lax.ppermute(x, "state", [(i, (i + k + 1) % shards) for i in range(shards)]) for k, x in enumerate(parts)
        ]

    *parts, held, weights, limits, beside = call(
        functools.partial(fetch_kernel, shards, width),
        ([group, half] if pair else [part] * (shards - 1)) + [jax.ShapeDtypeStruct(x.shape, x.dtype) for x in inputs],
        [HBM] * len(inputs),
        *inputs,
        scratch=[dma((4,))],
        flops=LONG,
        name="fetch",
    )
    if pair:
        leaving = parts[0]
        arrived_half = swapped(parts[1:])[0]
        near_halo = shifted(leaving, -1, across=True)
        kept = call(
            functools.partial(without, functools.partial(rotate_kernel, shards, width, 0, 0), 3, 1),
            [group, half],
            [VMEM] * 3 + [ANY],
            held,
            weights,
            limits,
            leaving,
            name="rotate_in",
        )
        far_halo = to_far_of_neighbor(kept[0])
    else:
        arrived = swapped(parts)
        kept = call(
            functools.partial(rotate_kernel, shards, width, 0, 0), [part], [VMEM] * 3, held, weights, limits, name="rotate_in"
        )
    table = call(
        functools.partial(without, functools.partial(table_kernel, elems * ring, shards, width), 2, 1),
        [jax.ShapeDtypeStruct((elems, couplings + 1, 8, 128), jnp.int32)],
        [VMEM, VMEM, ANY],
        beside,
        limits,
        kept[0],
        name="table",
    )[0]

    def pack(g, behind):
        return call(
            functools.partial(without, functools.partial(pack_kernel, shards, g), 1, 1),
            [bf16(width, rows, couplings * rows)],
            [VMEM, ANY],
            blocks,
            behind,
            name="pack",
        )[0]

    packed = {0: pack(0, table)}
    packed[2] = pack(2, packed[0])
    packed[1] = pack(1, packed[2])
    if pair:
        near = kept[0]
        middle, leaving = call(
            functools.partial(without, middle_kernel, 3, 1),
            [group] * 2,
            [VMEM] * 3 + [ANY],
            kept[1],
            arrived_half,
            leaving,
            packed[1],
            flops=SHORT,
            name="gather",
        )
        far = swapped([leaving])[0]
    else:
        near, middle, far = call(
            functools.partial(without, functools.partial(gather_kernel, shards), shards, 1),
            [group] * 3,
            [VMEM] * shards + [ANY],
            *kept,
            *arrived,
            packed[1],
            scratch=[whole],
            name="gather",
        )
        near_halo, far_halo = to_near_of_neighbor(far), to_far_of_neighbor(near)

    def level(g, m, before, here, after, previous, which=None, instead=None, split=False, behind=(), flops=0):
        body = functools.partial(level_kernel, g * width, 1.0 if m == 1 else 2.0, previous is not None)
        args = [packed[g], table, before, here, after] + ([] if previous is None else [previous])
        if which is not None:
            body = functools.partial(level_if_kernel, which, instead is not None, body, len(args))
            args += [] if instead is None else [instead]
        specs = [VMEM] * len(args)
        if behind:
            body = functools.partial(without, body, len(args), len(behind))
            args, specs = args + list(behind), specs + [ANY] * len(behind)
        outs = call(
            body,
            [group] + [half] * split,
            specs,
            *args,
            scratch=[pltpu.VMEM((3 * width, rows, lanes), jnp.bfloat16)],
            flops=flops,
            name=("near", "middle", "far")[g] + str(m),
        )
        return outs if split else outs[0]

    older = (None, None, None)
    for m in range(1, DEG + 1):
        last = m == DEG
        if m == 1:
            new_near = level(0, m, near_halo, near, middle, older[0])
            next_far_halo = to_far_of_neighbor(new_near)
            new_far = level(2, m, middle, far, far_halo, older[2], behind=[new_near])
            next_near_halo = to_near_of_neighbor(new_far)
            new_middle = level(1, m, near, middle, far, older[1])
        elif m % 2:
            new_middle = level(1, m, near, middle, far, older[1])
            new_near = level(0, m, near_halo, near, middle, older[0], behind=[new_middle])
            next_far_halo = to_far_of_neighbor(new_near)
            new_far = level(2, m, middle, far, far_halo, older[2], behind=[new_near])
            next_near_halo = to_near_of_neighbor(new_far)
        elif not last:
            new_far = level(2, m, middle, far, far_halo, older[2])
            next_near_halo = to_near_of_neighbor(new_far)
            new_middle = level(1, m, near, middle, far, older[1], behind=[new_far])
            new_near = level(0, m, near_halo, near, middle, older[0], behind=[new_middle])
            next_far_halo = to_far_of_neighbor(new_near)
        else:
            if pair:
                mate_halo = permuted(near, lambda i, j: (i ^ 1, j))
                early = level(2, m, middle, far, mate_halo, older[2], which=0)
                new_middle, half_leaving = level(1, m, near, middle, far, older[1], split=True, behind=[early])
                half_arrived = swapped([half_leaving])[0]
                new_far = level(2, m, middle, far, far_halo, older[2], which=1, instead=early)
                arrived = swapped([new_far])[0]
            else:
                new_middle = level(1, m, near, middle, far, older[1])
                new_far = level(2, m, middle, far, far_halo, older[2])
            behind = [half_arrived] if pair else []
            new_near = level(0, m, near_halo, near, middle, older[0], behind=behind, flops=LONG)
        if not last:
            near_halo, far_halo = next_near_halo, next_far_halo
        older, (near, middle, far) = (near, middle, far), (new_near, new_middle, new_far)

    whole_out = [bf16(*orbitals.shape)]
    if pair:
        out = call(
            own_kernel,
            whole_out,
            [VMEM] * 3,
            near,
            middle,
            half_arrived,
            out_specs=[HBM],
            scratch=[dma((3,))],
            name="own",
        )[0]
        return call(
            functools.partial(without, others_kernel, 1, 1),
            whole_out,
            [VMEM, HBM],
            arrived,
            out,
            out_specs=[HBM],
            scratch=[dma],
            aliases={1: 0},
            name="others",
        )[0]
    kept, *parts = call(
        functools.partial(scatter_kernel, shards),
        [part] * shards,
        [VMEM] * 3,
        near,
        middle,
        far,
        scratch=[whole],
        name="scatter",
    )
    return call(
        functools.partial(join_kernel, shards),
        whole_out,
        [VMEM] * shards,
        kept,
        *swapped(parts),
        out_specs=[HBM],
        scratch=[dma((shards,))],
        name="join",
    )[0]


def solution(mesh):
    in_specs = (
        P(("elem", "state"), None, None),
        P(),
        P("elem"),
        P("elem", None),
        P("elem", None, None, None),
    )
    out_specs = P(("elem", "state"), None, None)
    return jax.shard_map(on_device, mesh=mesh, in_specs=in_specs, out_specs=out_specs, check_vma=False)
```

```python
import functools

import jax
import jax.numpy as jnp
from jax import lax
from jax.experimental import pallas as pl
from jax.experimental.pallas import tpu as pltpu
from jax.sharding import PartitionSpec as P

DEG = 4
FULL = 128
DEPTH = 512
LONG, SHORT = 20 * 10**9, 10**9

center_shift = 0.2
half_span = 1.1

VMEM = pl.BlockSpec(memory_space=pltpu.VMEM)
HBM = pl.BlockSpec(memory_space=pltpu.HBM)
ANY = pl.BlockSpec(memory_space=pl.ANY)


def call(kernel, outs, ins, *args, out_specs=None, scratch=(), aliases=None, limit=4 << 20, flops=0, name=None):
    return pl.pallas_call(
        kernel,
        out_shape=outs,
        in_specs=ins,
        out_specs=out_specs or [VMEM] * len(outs),
        scratch_shapes=list(scratch),
        input_output_aliases=aliases or {},
        compiler_params=pltpu.CompilerParams(vmem_limit_bytes=limit),
        cost_estimate=pl.CostEstimate(flops=flops, bytes_accessed=1024, transcendentals=0),
        name=name,
    )(*args)


def bf16(*shape):
    return jax.ShapeDtypeStruct(shape, jnp.bfloat16)


def without(body, at, count, *refs):
    body(*refs[:at], *refs[at + count :])


def flipped(shards):
    return lax.axis_index("state") == 1 if shards == 2 else False


def choose(flip, yes, no):
    return no if flip is False else jnp.where(flip, yes, no)


def rows_below(count, rows, lanes):
    return lax.broadcasted_iota(jnp.int32, (rows, lanes), 0) < count


def turn(shards, k, element, weights, count):
    rows, lanes = element.shape[0], weights.shape[1] // shards
    at = lax.rem(lax.axis_index("state") + k, shards) * lanes
    turned = jnp.dot(element, weights[:, pl.ds(pl.multiple_of(at, lanes), lanes)], preferred_element_type=jnp.float32)
    return jnp.where(rows_below(count, rows, lanes), turned, 0.0).astype(jnp.bfloat16)


def rotate_kernel(shards, reach, k, first, held, weights, limits, *outs):
    me, flip = lax.axis_index("state"), flipped(shards)
    elems = held.shape[0]
    ends = limits[...]
    spots = [(out, e) for out in outs for e in range(out.shape[0])]
    for spot, (out, at) in enumerate(spots, first):
        e = choose(flip, (spot + elems - reach) % elems, spot)
        count = ends[spot]
        for shard in range(shards):
            here = (spot + elems - reach) % elems if shard == 1 and flip is not False else spot
            count = jnp.where(me == shard, ends[shard * elems + here], count)
        out[at] = turn(shards, k, held[e], weights, count)


def fetch_kernel(shards, reach, orbitals, rotation, counts, neighbors, *refs):
    outs, (held, weights, limits, beside, sems) = refs[:-5], refs[-5:]
    copies = [
        pltpu.make_async_copy(source, target, sems.at[i])
        for i, (source, target) in enumerate(
            [(rotation, weights), (counts, limits), (orbitals, held), (neighbors, beside)]
        )
    ]
    for copy in copies:
        copy.start()
    for copy in copies[:3]:
        copy.wait()
    if shards == 2:
        near, half = outs
        rotate_kernel(shards, reach, 1, reach, held, weights, limits, half)
        rotate_kernel(shards, reach, 1, 0, held, weights, limits, near)
    else:
        for k, out in enumerate(outs):
            rotate_kernel(shards, reach, k + 1, 0, held, weights, limits, out)
    copies[3].wait()


def table_kernel(total, shards, reach, beside, limits, table):
    couplings, elems = beside.shape
    flip, groups = flipped(shards), elems // reach
    column = lax.broadcasted_iota(jnp.int32, beside.shape, 1)
    offset = beside[...] - (column + lax.axis_index("elem") * elems)
    offset = jnp.where(offset > reach, offset - total, jnp.where(offset < -reach, offset + total, offset))
    place = offset + (column - sum(jnp.where(column >= g * reach, reach, 0) for g in range(1, groups))) + reach
    past = sum(jnp.where(place >= g * reach, reach, 0) for g in range(1, groups))
    place = choose(flip, place + (elems - reach) - 2 * past, place)
    ends = limits[...].reshape(1, elems)

    def mirrored(x):
        parts = [x[:, g * reach : (g + 1) * reach] for g in reversed(range(groups))]
        return choose(flip, jnp.concatenate(parts, axis=1), x)

    rows = jnp.concatenate([mirrored(place), mirrored(ends)], axis=0)
    for e in range(elems):
        for k in range(couplings + 1):
            table[e, k] = jnp.full(table.shape[2:], rows[k, e], jnp.int32)


def pack_kernel(shards, group, blocks, packed):
    elems, couplings, _, _ = blocks.shape
    width = packed.shape[0]
    first = choose(flipped(shards), elems - (group + 1) * width, group * width)
    for e in range(width):
        for k in range(couplings):
            packed[e, :, k * FULL : (k + 1) * FULL] = blocks[first + e, k, :, :FULL]
        tail = [blocks[first + e, k, :, FULL:] for k in range(couplings)]
        packed[e, :, couplings * FULL :] = jnp.concatenate(tail, axis=1)


def middle_kernel(half, arrived, leaving, middle, copied):
    flip, share = flipped(2), half.shape[0]
    copied[...] = leaving[...]
    middle[pl.ds(choose(flip, share, 0), share)] = half[...]
    middle[pl.ds(choose(flip, 0, share), share)] = arrived[...]


def gather_kernel(shards, *refs):
    me = lax.axis_index("state")
    parts, groups, whole = refs[:shards], refs[shards : shards + 3], refs[-1]
    elems, width = parts[0].shape[0], groups[0].shape[0]
    for k, part in enumerate(parts):
        whole[pl.ds(lax.rem(me + shards - k, shards) * elems, elems)] = part[...]
    for g, group in enumerate(groups):
        group[...] = whole[g * width : (g + 1) * width]


def hard():
    return lax.rem(lax.axis_index("elem") + lax.axis_index("state"), 2)


def level_if_kernel(which, instead, body, at, *refs):
    if instead:
        other, refs = refs[at], refs[:at] + refs[at + 1 :]

        @pl.when(hard() != which)
        def _():
            refs[-2][...] = other[...]

    pl.when(hard() == which)(functools.partial(body, *refs))


def level_kernel(first, factor, with_prev, packed, table, before, here, after, *refs):
    refs, window = list(refs[:-1]), refs[-1]
    previous = refs.pop(0) if with_prev else None
    out = refs[0]
    width, rows, lanes = here.shape
    for g, group in enumerate((before, here, after)):
        window[g * width : (g + 1) * width] = group[...]
    couplings = table.shape[1] - 1
    for e in range(width):
        *at, end = [table[first + e, k, 0, 0] for k in range(couplings + 1)]
        fields = jnp.concatenate([window[i, :FULL] for i in at] + [window[i, FULL:] for i in at], axis=0)
        image = jnp.zeros((rows, lanes), jnp.float32)
        for k in range(0, fields.shape[0], DEPTH):
            part = packed[e, :, k : k + DEPTH]
            image += jnp.dot(part, fields[k : k + DEPTH], preferred_element_type=jnp.float32)
        image = jnp.where(rows_below(end, rows, lanes), image, 0.0)
        value = factor * (image - center_shift * here[e].astype(jnp.float32)) / half_span
        if with_prev:
            value = value - previous[e].astype(jnp.float32)
        out[e] = value.astype(jnp.bfloat16)
    if len(refs) > 1:
        share = refs[1].shape[0]
        refs[1][...] = out[pl.ds(choose(flipped(2), 0, width - share), share)]


def scatter_kernel(shards, *refs):
    me = lax.axis_index("state")
    groups, parts, whole = refs[:3], refs[3:-1], refs[-1]
    elems, width = parts[0].shape[0], groups[0].shape[0]
    for g, group in enumerate(groups):
        whole[g * width : (g + 1) * width] = group[...]
    for k, part in enumerate(parts):
        part[...] = whole[pl.ds(lax.rem(me + k, shards) * elems, elems)]


def place(shards, k, first, part, out, sem):
    elems, _, lanes = part.shape
    at = lax.rem(lax.axis_index("state") + shards - k, shards) * lanes
    return pltpu.make_async_copy(part, out.at[pl.ds(first, elems), :, pl.ds(pl.multiple_of(at, lanes), lanes)], sem)


def run(copies):
    for copy in copies:
        copy.start()
    for copy in copies:
        copy.wait()


def near_copy(k, near, out, sem):
    return place(2, k, choose(flipped(2), out.shape[0] - near.shape[0], 0), near, out, sem)


def half_copy(k, half, out, sem):
    return place(2, k, choose(flipped(2), 0, out.shape[0] - half.shape[0]), half, out, sem)


def own_kernel(near, middle, half, out, sems):
    share = half.shape[0]
    kept = middle.at[pl.ds(choose(flipped(2), share, 0), share)]
    run([near_copy(0, near, out, sems.at[0]), half_copy(0, kept, out, sems.at[1]), half_copy(1, half, out, sems.at[2])])


def others_kernel(far, out, sem):
    run([near_copy(1, far, out, sem)])


def join_kernel(shards, *refs):
    parts, out, sems = refs[:shards], refs[-2], refs[-1]
    run([place(shards, k, 0, part, out, sems.at[k]) for k, part in enumerate(parts)])


def on_device(orbitals, rotation, counts, neighbors, blocks):
    row_elems, rows, states = orbitals.shape
    elems, couplings = neighbors.shape
    inputs = [
        pltpu.with_memory_space_constraint(x, pltpu.HBM) for x in (orbitals, rotation, counts, neighbors.T)
    ]
    shards = lax.axis_size("state")
    ring = lax.axis_size("elem")
    width = elems // 3
    lanes = states // shards
    group, part = bf16(width, rows, lanes), bf16(row_elems, rows, lanes)
    half = bf16(row_elems - width, rows, lanes)
    whole = pltpu.VMEM((elems, rows, lanes), jnp.bfloat16)
    dma = pltpu.SemaphoreType.DMA
    pair = shards == 2

    def permuted(x, target):
        moves = []
        for i in range(ring):
            for j in range(shards):
                to_i, to_j = target(i, j)
                moves.append((i * shards + j, to_i % ring * shards + to_j))
        return lax.ppermute(x, ("elem", "state"), moves)

    def shifted(x, step, across=False):
        return permuted(x, lambda i, j: (i + (-step if pair and j == 1 else step), 1 - j if across else j))

    def to_far_of_neighbor(x):
        return shifted(x, -1)

    def to_near_of_neighbor(x):
        return shifted(x, 1)

    def swapped(parts):
        return [
            lax.ppermute(x, "state", [(i, (i + k + 1) % shards) for i in range(shards)]) for k, x in enumerate(parts)
        ]

    *parts, held, weights, limits, beside = call(
        functools.partial(fetch_kernel, shards, width),
        ([group, half] if pair else [part] * (shards - 1)) + [jax.ShapeDtypeStruct(x.shape, x.dtype) for x in inputs],
        [HBM] * len(inputs),
        *inputs,
        scratch=[dma((4,))],
        flops=LONG,
        name="fetch",
    )
    if pair:
        leaving = parts[0]
        arrived_half = swapped(parts[1:])[0]
        near_halo = shifted(leaving, -1, across=True)
        kept = call(
            functools.partial(without, functools.partial(rotate_kernel, shards, width, 0, 0), 3, 1),
            [group, half],
            [VMEM] * 3 + [ANY],
            held,
            weights,
            limits,
            leaving,
            name="rotate_in",
        )
        far_halo = to_far_of_neighbor(kept[0])
    else:
        arrived = swapped(parts)
        kept = call(
            functools.partial(rotate_kernel, shards, width, 0, 0), [part], [VMEM] * 3, held, weights, limits, name="rotate_in"
        )
    table = call(
        functools.partial(without, functools.partial(table_kernel, elems * ring, shards, width), 2, 1),
        [jax.ShapeDtypeStruct((elems, couplings + 1, 8, 128), jnp.int32)],
        [VMEM, VMEM, ANY],
        beside,
        limits,
        kept[0],
        name="table",
    )[0]

    def pack(g, behind):
        return call(
            functools.partial(without, functools.partial(pack_kernel, shards, g), 1, 1),
            [bf16(width, rows, couplings * rows)],
            [VMEM, ANY],
            blocks,
            behind,
            name="pack",
        )[0]

    packed = {0: pack(0, table)}
    packed[2] = pack(2, packed[0])
    packed[1] = pack(1, packed[2])
    if pair:
        near = kept[0]
        middle, leaving = call(
            functools.partial(without, middle_kernel, 3, 1),
            [group] * 2,
            [VMEM] * 3 + [ANY],
            kept[1],
            arrived_half,
            leaving,
            packed[1],
            flops=SHORT,
            name="gather",
        )
        far = swapped([leaving])[0]
    else:
        near, middle, far = call(
            functools.partial(without, functools.partial(gather_kernel, shards), shards, 1),
            [group] * 3,
            [VMEM] * shards + [ANY],
            *kept,
            *arrived,
            packed[1],
            scratch=[whole],
            name="gather",
        )
        near_halo, far_halo = to_near_of_neighbor(far), to_far_of_neighbor(near)

    def level(g, m, before, here, after, previous, which=None, instead=None, split=False, behind=(), flops=0):
        body = functools.partial(level_kernel, g * width, 1.0 if m == 1 else 2.0, previous is not None)
        args = [packed[g], table, before, here, after] + ([] if previous is None else [previous])
        if which is not None:
            body = functools.partial(level_if_kernel, which, instead is not None, body, len(args))
            args += [] if instead is None else [instead]
        specs = [VMEM] * len(args)
        if behind:
            body = functools.partial(without, body, len(args), len(behind))
            args, specs = args + list(behind), specs + [ANY] * len(behind)
        outs = call(
            body,
            [group] + [half] * split,
            specs,
            *args,
            scratch=[pltpu.VMEM((3 * width, rows, lanes), jnp.bfloat16)],
            flops=flops,
            name=("near", "middle", "far")[g] + str(m),
        )
        return outs if split else outs[0]

    older = (None, None, None)
    for m in range(1, DEG + 1):
        last = m == DEG
        if m == 1:
            new_near = level(0, m, near_halo, near, middle, older[0])
            next_far_halo = to_far_of_neighbor(new_near)
            new_far = level(2, m, middle, far, far_halo, older[2], behind=[new_near])
            next_near_halo = to_near_of_neighbor(new_far)
            new_middle = level(1, m, near, middle, far, older[1])
        elif m % 2:
            new_middle = level(1, m, near, middle, far, older[1])
            new_near = level(0, m, near_halo, near, middle, older[0], behind=[new_middle])
            next_far_halo = to_far_of_neighbor(new_near)
            new_far = level(2, m, middle, far, far_halo, older[2], behind=[new_near])
            next_near_halo = to_near_of_neighbor(new_far)
        elif not last:
            new_far = level(2, m, middle, far, far_halo, older[2])
            next_near_halo = to_near_of_neighbor(new_far)
            new_middle = level(1, m, near, middle, far, older[1], behind=[new_far])
            new_near = level(0, m, near_halo, near, middle, older[0], behind=[new_middle])
            next_far_halo = to_far_of_neighbor(new_near)
        else:
            if pair:
                mate_halo = permuted(near, lambda i, j: (i ^ 1, j))
                early = level(2, m, middle, far, mate_halo, older[2], which=0)
                new_middle, half_leaving = level(1, m, near, middle, far, older[1], split=True, behind=[early])
                half_arrived = swapped([half_leaving])[0]
                new_far = level(2, m, middle, far, far_halo, older[2], which=1, instead=early)
                arrived = swapped([new_far])[0]
            else:
                new_middle = level(1, m, near, middle, far, older[1])
                new_far = level(2, m, middle, far, far_halo, older[2])
            behind = [half_arrived] if pair else []
            new_near = level(0, m, near_halo, near, middle, older[0], behind=behind, flops=LONG)
        if not last:
            near_halo, far_halo = next_near_halo, next_far_halo
        older, (near, middle, far) = (near, middle, far), (new_near, new_middle, new_far)

    whole_out = [bf16(*orbitals.shape)]
    if pair:
        out = call(
            own_kernel,
            whole_out,
            [VMEM] * 3,
            near,
            middle,
            half_arrived,
            out_specs=[HBM],
            scratch=[dma((3,))],
            name="own",
        )[0]
        return call(
            functools.partial(without, others_kernel, 1, 1),
            whole_out,
            [VMEM, HBM],
            arrived,
            out,
            out_specs=[HBM],
            scratch=[dma],
            aliases={1: 0},
            name="others",
        )[0]
    kept, *parts = call(
        functools.partial(scatter_kernel, shards),
        [part] * shards,
        [VMEM] * 3,
        near,
        middle,
        far,
        scratch=[whole],
        name="scatter",
    )
    return call(
        functools.partial(join_kernel, shards),
        whole_out,
        [VMEM] * shards,
        kept,
        *swapped(parts),
        out_specs=[HBM],
        scratch=[dma((shards,))],
        name="join",
    )[0]


def solution(mesh):
    in_specs = (
        P(("elem", "state"), None, None),
        P(),
        P("elem"),
        P("elem", None),
        P("elem", None, None, None),
    )
    out_specs = P(("elem", "state"), None, None)
    return jax.shard_map(on_device, mesh=mesh, in_specs=in_specs, out_specs=out_specs, check_vma=False)
```

```python
import functools

import jax
import jax.numpy as jnp
from jax import lax
from jax.experimental import pallas as pl
from jax.experimental.pallas import tpu as pltpu
from jax.sharding import PartitionSpec as P

DEG = 4
FULL = 128
DEPTH = 512
LONG, SHORT = 20 * 10**9, 10**9

center_shift = 0.2
half_span = 1.1

VMEM = pl.BlockSpec(memory_space=pltpu.VMEM)
HBM = pl.BlockSpec(memory_space=pltpu.HBM)
ANY = pl.BlockSpec(memory_space=pl.ANY)


def call(kernel, outs, ins, *args, out_specs=None, scratch=(), aliases=None, limit=4 << 20, flops=0, name=None):
    return pl.pallas_call(
        kernel,
        out_shape=outs,
        in_specs=ins,
        out_specs=out_specs or [VMEM] * len(outs),
        scratch_shapes=list(scratch),
        input_output_aliases=aliases or {},
        compiler_params=pltpu.CompilerParams(vmem_limit_bytes=limit),
        cost_estimate=pl.CostEstimate(flops=flops, bytes_accessed=1024, transcendentals=0),
        name=name,
    )(*args)


def bf16(*shape):
    return jax.ShapeDtypeStruct(shape, jnp.bfloat16)


def without(body, at, count, *refs):
    body(*refs[:at], *refs[at + count :])


def flipped(shards):
    return lax.axis_index("state") == 1 if shards == 2 else False


def choose(flip, yes, no):
    return no if flip is False else jnp.where(flip, yes, no)


def rows_below(count, rows, lanes):
    return lax.broadcasted_iota(jnp.int32, (rows, lanes), 0) < count


def turn(shards, k, element, weights, count):
    rows, lanes = element.shape[0], weights.shape[1] // shards
    at = lax.rem(lax.axis_index("state") + k, shards) * lanes
    turned = jnp.dot(element, weights[:, pl.ds(pl.multiple_of(at, lanes), lanes)], preferred_element_type=jnp.float32)
    return jnp.where(rows_below(count, rows, lanes), turned, 0.0).astype(jnp.bfloat16)


def rotate_kernel(shards, reach, k, first, held, weights, limits, *outs):
    me, flip = lax.axis_index("state"), flipped(shards)
    elems = held.shape[0]
    ends = limits[...]
    spots = [(out, e) for out in outs for e in range(out.shape[0])]
    for spot, (out, at) in enumerate(spots, first):
        e = choose(flip, (spot + elems - reach) % elems, spot)
        count = ends[spot]
        for shard in range(shards):
            here = (spot + elems - reach) % elems if shard == 1 and flip is not False else spot
            count = jnp.where(me == shard, ends[shard * elems + here], count)
        out[at] = turn(shards, k, held[e], weights, count)


def fetch_kernel(shards, reach, orbitals, rotation, counts, neighbors, *refs):
    outs, (held, weights, limits, beside, sems) = refs[:-5], refs[-5:]
    copies = [
        pltpu.make_async_copy(source, target, sems.at[i])
        for i, (source, target) in enumerate(
            [(rotation, weights), (counts, limits), (orbitals, held), (neighbors, beside)]
        )
    ]
    for copy in copies:
        copy.start()
    for copy in copies[:3]:
        copy.wait()
    if shards == 2:
        near, half = outs
        rotate_kernel(shards, reach, 1, reach, held, weights, limits, half)
        rotate_kernel(shards, reach, 1, 0, held, weights, limits, near)
    else:
        for k, out in enumerate(outs):
            rotate_kernel(shards, reach, k + 1, 0, held, weights, limits, out)
    copies[3].wait()


def copy_kernel(source, target):
    target[...] = source[...]


def table_kernel(total, shards, reach, beside, limits, table):
    couplings, elems = beside.shape
    flip, groups = flipped(shards), elems // reach
    column = lax.broadcasted_iota(jnp.int32, beside.shape, 1)
    offset = beside[...] - (column + lax.axis_index("elem") * elems)
    offset = jnp.where(offset > reach, offset - total, jnp.where(offset < -reach, offset + total, offset))
    place = offset + (column - sum(jnp.where(column >= g * reach, reach, 0) for g in range(1, groups))) + reach
    past = sum(jnp.where(place >= g * reach, reach, 0) for g in range(1, groups))
    place = choose(flip, place + (elems - reach) - 2 * past, place)
    ends = limits[...].reshape(1, elems)

    def mirrored(x):
        parts = [x[:, g * reach : (g + 1) * reach] for g in reversed(range(groups))]
        return choose(flip, jnp.concatenate(parts, axis=1), x)

    rows = jnp.concatenate([mirrored(place), mirrored(ends)], axis=0)
    for e in range(elems):
        for k in range(couplings + 1):
            table[e, k] = jnp.full(table.shape[2:], rows[k, e], jnp.int32)


def pack_kernel(shards, group, blocks, packed):
    elems, couplings, _, _ = blocks.shape
    width = packed.shape[0]
    first = choose(flipped(shards), elems - (group + 1) * width, group * width)
    for e in range(width):
        for k in range(couplings):
            packed[e, :, k * FULL : (k + 1) * FULL] = blocks[first + e, k, :, :FULL]
        tail = [blocks[first + e, k, :, FULL:] for k in range(couplings)]
        packed[e, :, couplings * FULL :] = jnp.concatenate(tail, axis=1)


def middle_kernel(half, arrived, leaving, middle, copied):
    flip, share = flipped(2), half.shape[0]
    copied[...] = leaving[...]
    middle[pl.ds(choose(flip, share, 0), share)] = half[...]
    middle[pl.ds(choose(flip, 0, share), share)] = arrived[...]


def gather_kernel(shards, *refs):
    me = lax.axis_index("state")
    parts, groups, whole = refs[:shards], refs[shards : shards + 3], refs[-1]
    elems, width = parts[0].shape[0], groups[0].shape[0]
    for k, part in enumerate(parts):
        whole[pl.ds(lax.rem(me + shards - k, shards) * elems, elems)] = part[...]
    for g, group in enumerate(groups):
        group[...] = whole[g * width : (g + 1) * width]


def hard():
    return lax.rem(lax.axis_index("elem") + lax.axis_index("state"), 2)


def level_if_kernel(which, instead, body, at, *refs):
    if instead:
        other, refs = refs[at], refs[:at] + refs[at + 1 :]

        @pl.when(hard() != which)
        def _():
            refs[-2][...] = other[...]

    pl.when(hard() == which)(functools.partial(body, *refs))


def level_kernel(first, factor, with_prev, packed, table, before, here, after, *refs):
    refs, window = list(refs[:-1]), refs[-1]
    previous = refs.pop(0) if with_prev else None
    out = refs[0]
    width, rows, lanes = here.shape
    for g, group in enumerate((before, here, after)):
        window[g * width : (g + 1) * width] = group[...]
    couplings = table.shape[1] - 1
    for e in range(width):
        *at, end = [table[first + e, k, 0, 0] for k in range(couplings + 1)]
        fields = jnp.concatenate([window[i, :FULL] for i in at] + [window[i, FULL:] for i in at], axis=0)
        image = jnp.zeros((rows, lanes), jnp.float32)
        for k in range(0, fields.shape[0], DEPTH):
            part = packed[e, :, k : k + DEPTH]
            image += jnp.dot(part, fields[k : k + DEPTH], preferred_element_type=jnp.float32)
        image = jnp.where(rows_below(end, rows, lanes), image, 0.0)
        value = factor * (image - center_shift * here[e].astype(jnp.float32)) / half_span
        if with_prev:
            value = value - previous[e].astype(jnp.float32)
        out[e] = value.astype(jnp.bfloat16)
    if len(refs) > 1:
        share = refs[1].shape[0]
        refs[1][...] = out[pl.ds(choose(flipped(2), 0, width - share), share)]


def scatter_kernel(shards, *refs):
    me = lax.axis_index("state")
    groups, parts, whole = refs[:3], refs[3:-1], refs[-1]
    elems, width = parts[0].shape[0], groups[0].shape[0]
    for g, group in enumerate(groups):
        whole[g * width : (g + 1) * width] = group[...]
    for k, part in enumerate(parts):
        part[...] = whole[pl.ds(lax.rem(me + k, shards) * elems, elems)]


def place(shards, k, first, part, out, sem):
    elems, _, lanes = part.shape
    at = lax.rem(lax.axis_index("state") + shards - k, shards) * lanes
    return pltpu.make_async_copy(part, out.at[pl.ds(first, elems), :, pl.ds(pl.multiple_of(at, lanes), lanes)], sem)


def run(copies):
    for copy in copies:
        copy.start()
    for copy in copies:
        copy.wait()


def near_copy(k, near, out, sem):
    return place(2, k, choose(flipped(2), out.shape[0] - near.shape[0], 0), near, out, sem)


def half_copy(k, half, out, sem):
    return place(2, k, choose(flipped(2), 0, out.shape[0] - half.shape[0]), half, out, sem)


def own_kernel(near, middle, half, out, sems):
    share = half.shape[0]
    kept = middle.at[pl.ds(choose(flipped(2), share, 0), share)]
    run([near_copy(0, near, out, sems.at[0]), half_copy(0, kept, out, sems.at[1]), half_copy(1, half, out, sems.at[2])])


def others_kernel(far, out, sem):
    run([near_copy(1, far, out, sem)])


def join_kernel(shards, *refs):
    parts, out, sems = refs[:shards], refs[-2], refs[-1]
    run([place(shards, k, 0, part, out, sems.at[k]) for k, part in enumerate(parts)])


def on_device(orbitals, rotation, counts, neighbors, blocks):
    row_elems, rows, states = orbitals.shape
    elems, couplings = neighbors.shape
    inputs = [
        pltpu.with_memory_space_constraint(x, pltpu.HBM) for x in (orbitals, rotation, counts, neighbors.T)
    ]
    shards = lax.axis_size("state")
    ring = lax.axis_size("elem")
    width = elems // 3
    lanes = states // shards
    group, part = bf16(width, rows, lanes), bf16(row_elems, rows, lanes)
    half = bf16(row_elems - width, rows, lanes)
    whole = pltpu.VMEM((elems, rows, lanes), jnp.bfloat16)
    dma = pltpu.SemaphoreType.DMA
    pair = shards == 2

    def permuted(x, target):
        moves = []
        for i in range(ring):
            for j in range(shards):
                to_i, to_j = target(i, j)
                moves.append((i * shards + j, to_i % ring * shards + to_j))
        return lax.ppermute(x, ("elem", "state"), moves)

    def shifted(x, step, across=False):
        return permuted(x, lambda i, j: (i + (-step if pair and j == 1 else step), 1 - j if across else j))

    def to_far_of_neighbor(x):
        return shifted(x, -1)

    def to_near_of_neighbor(x):
        return shifted(x, 1)

    def swapped(parts):
        return [
            lax.ppermute(x, "state", [(i, (i + k + 1) % shards) for i in range(shards)]) for k, x in enumerate(parts)
        ]

    *parts, held, weights, limits, beside = call(
        functools.partial(fetch_kernel, shards, width),
        ([group, half] if pair else [part] * (shards - 1)) + [jax.ShapeDtypeStruct(x.shape, x.dtype) for x in inputs],
        [HBM] * len(inputs),
        *inputs,
        scratch=[dma((4,))],
        name="fetch",
    )
    if pair:
        leaving = call(copy_kernel, [group], [VMEM], parts[0], flops=LONG, name="copy")[0]
        arrived_half = swapped(parts[1:])[0]
        near_halo = shifted(leaving, -1, across=True)
        kept = call(
            functools.partial(without, functools.partial(rotate_kernel, shards, width, 0, 0), 3, 1),
            [group, half],
            [VMEM] * 3 + [ANY],
            held,
            weights,
            limits,
            leaving,
            name="rotate_in",
        )
        far_halo = to_far_of_neighbor(kept[0])
    else:
        arrived = swapped(parts)
        kept = call(
            functools.partial(rotate_kernel, shards, width, 0, 0), [part], [VMEM] * 3, held, weights, limits, name="rotate_in"
        )
    table = call(
        functools.partial(without, functools.partial(table_kernel, elems * ring, shards, width), 2, 1),
        [jax.ShapeDtypeStruct((elems, couplings + 1, 8, 128), jnp.int32)],
        [VMEM, VMEM, ANY],
        beside,
        limits,
        kept[0],
        name="table",
    )[0]

    def pack(g, behind):
        return call(
            functools.partial(without, functools.partial(pack_kernel, shards, g), 1, 1),
            [bf16(width, rows, couplings * rows)],
            [VMEM, ANY],
            blocks,
            behind,
            name="pack",
        )[0]

    packed = {0: pack(0, table)}
    packed[2] = pack(2, packed[0])
    packed[1] = pack(1, packed[2])
    if pair:
        near = kept[0]
        middle, leaving = call(
            functools.partial(without, middle_kernel, 3, 1),
            [group] * 2,
            [VMEM] * 3 + [ANY],
            kept[1],
            arrived_half,
            leaving,
            packed[1],
            flops=SHORT,
            name="gather",
        )
        far = swapped([leaving])[0]
    else:
        near, middle, far = call(
            functools.partial(without, functools.partial(gather_kernel, shards), shards, 1),
            [group] * 3,
            [VMEM] * shards + [ANY],
            *kept,
            *arrived,
            packed[1],
            scratch=[whole],
            name="gather",
        )
        near_halo, far_halo = to_near_of_neighbor(far), to_far_of_neighbor(near)

    def level(g, m, before, here, after, previous, which=None, instead=None, split=False, behind=(), flops=0):
        body = functools.partial(level_kernel, g * width, 1.0 if m == 1 else 2.0, previous is not None)
        args = [packed[g], table, before, here, after] + ([] if previous is None else [previous])
        if which is not None:
            body = functools.partial(level_if_kernel, which, instead is not None, body, len(args))
            args += [] if instead is None else [instead]
        specs = [VMEM] * len(args)
        if behind:
            body = functools.partial(without, body, len(args), len(behind))
            args, specs = args + list(behind), specs + [ANY] * len(behind)
        outs = call(
            body,
            [group] + [half] * split,
            specs,
            *args,
            scratch=[pltpu.VMEM((3 * width, rows, lanes), jnp.bfloat16)],
            flops=flops,
            name=("near", "middle", "far")[g] + str(m),
        )
        return outs if split else outs[0]

    older = (None, None, None)
    for m in range(1, DEG + 1):
        last = m == DEG
        if m == 1:
            new_near = level(0, m, near_halo, near, middle, older[0])
            next_far_halo = to_far_of_neighbor(new_near)
            new_far = level(2, m, middle, far, far_halo, older[2], behind=[new_near])
            next_near_halo = to_near_of_neighbor(new_far)
            new_middle = level(1, m, near, middle, far, older[1])
        elif m % 2:
            new_middle = level(1, m, near, middle, far, older[1])
            new_near = level(0, m, near_halo, near, middle, older[0], behind=[new_middle])
            next_far_halo = to_far_of_neighbor(new_near)
            new_far = level(2, m, middle, far, far_halo, older[2], behind=[new_near])
            next_near_halo = to_near_of_neighbor(new_far)
        elif not last:
            new_far = level(2, m, middle, far, far_halo, older[2])
            next_near_halo = to_near_of_neighbor(new_far)
            new_middle = level(1, m, near, middle, far, older[1], behind=[new_far])
            new_near = level(0, m, near_halo, near, middle, older[0], behind=[new_middle])
            next_far_halo = to_far_of_neighbor(new_near)
        else:
            if pair:
                mate_halo = permuted(near, lambda i, j: (i ^ 1, j))
                early = level(2, m, middle, far, mate_halo, older[2], which=0)
                new_middle, half_leaving = level(1, m, near, middle, far, older[1], split=True, behind=[early])
                half_arrived = swapped([half_leaving])[0]
                new_far = level(2, m, middle, far, far_halo, older[2], which=1, instead=early)
                arrived = swapped([new_far])[0]
            else:
                new_middle = level(1, m, near, middle, far, older[1])
                new_far = level(2, m, middle, far, far_halo, older[2])
            behind = [half_arrived] if pair else []
            new_near = level(0, m, near_halo, near, middle, older[0], behind=behind, flops=LONG)
        if not last:
            near_halo, far_halo = next_near_halo, next_far_halo
        older, (near, middle, far) = (near, middle, far), (new_near, new_middle, new_far)

    whole_out = [bf16(*orbitals.shape)]
    if pair:
        out = call(
            own_kernel,
            whole_out,
            [VMEM] * 3,
            near,
            middle,
            half_arrived,
            out_specs=[HBM],
            scratch=[dma((3,))],
            name="own",
        )[0]
        return call(
            functools.partial(without, others_kernel, 1, 1),
            whole_out,
            [VMEM, HBM],
            arrived,
            out,
            out_specs=[HBM],
            scratch=[dma],
            aliases={1: 0},
            name="others",
        )[0]
    kept, *parts = call(
        functools.partial(scatter_kernel, shards),
        [part] * shards,
        [VMEM] * 3,
        near,
        middle,
        far,
        scratch=[whole],
        name="scatter",
    )
    return call(
        functools.partial(join_kernel, shards),
        whole_out,
        [VMEM] * shards,
        kept,
        *swapped(parts),
        out_specs=[HBM],
        scratch=[dma((shards,))],
        name="join",
    )[0]


def solution(mesh):
    in_specs = (
        P(("elem", "state"), None, None),
        P(),
        P("elem"),
        P("elem", None),
        P("elem", None, None, None),
    )
    out_specs = P(("elem", "state"), None, None)
    return jax.shard_map(on_device, mesh=mesh, in_specs=in_specs, out_specs=out_specs, check_vma=False)
```

```python
import functools

import jax
import jax.numpy as jnp
from jax import lax
from jax.experimental import pallas as pl
from jax.experimental.pallas import tpu as pltpu
from jax.sharding import PartitionSpec as P

DEG = 4
FULL = 128
DEPTH = 512
LONG, SHORT = 20 * 10**9, 10**9

center_shift = 0.2
half_span = 1.1

VMEM = pl.BlockSpec(memory_space=pltpu.VMEM)
HBM = pl.BlockSpec(memory_space=pltpu.HBM)
ANY = pl.BlockSpec(memory_space=pl.ANY)


def call(kernel, outs, ins, *args, out_specs=None, scratch=(), aliases=None, limit=4 << 20, flops=0, name=None):
    return pl.pallas_call(
        kernel,
        out_shape=outs,
        in_specs=ins,
        out_specs=out_specs or [VMEM] * len(outs),
        scratch_shapes=list(scratch),
        input_output_aliases=aliases or {},
        compiler_params=pltpu.CompilerParams(vmem_limit_bytes=limit),
        cost_estimate=pl.CostEstimate(flops=flops, bytes_accessed=1024, transcendentals=0),
        name=name,
    )(*args)


def bf16(*shape):
    return jax.ShapeDtypeStruct(shape, jnp.bfloat16)


def without(body, at, count, *refs):
    body(*refs[:at], *refs[at + count :])


def flipped(shards):
    return lax.axis_index("state") == 1 if shards == 2 else False


def choose(flip, yes, no):
    return no if flip is False else jnp.where(flip, yes, no)


def rows_below(count, rows, lanes):
    return lax.broadcasted_iota(jnp.int32, (rows, lanes), 0) < count


def turn(shards, k, element, weights, count):
    rows, lanes = element.shape[0], weights.shape[1] // shards
    at = lax.rem(lax.axis_index("state") + k, shards) * lanes
    turned = jnp.dot(element, weights[:, pl.ds(pl.multiple_of(at, lanes), lanes)], preferred_element_type=jnp.float32)
    return jnp.where(rows_below(count, rows, lanes), turned, 0.0).astype(jnp.bfloat16)


def rotate_kernel(shards, reach, k, first, held, weights, limits, *outs):
    me, flip = lax.axis_index("state"), flipped(shards)
    elems = held.shape[0]
    ends = limits[...]
    spots = [(out, e) for out in outs for e in range(out.shape[0])]
    for spot, (out, at) in enumerate(spots, first):
        e = choose(flip, (spot + elems - reach) % elems, spot)
        count = ends[spot]
        for shard in range(shards):
            here = (spot + elems - reach) % elems if shard == 1 and flip is not False else spot
            count = jnp.where(me == shard, ends[shard * elems + here], count)
        out[at] = turn(shards, k, held[e], weights, count)


def fetch_kernel(shards, reach, orbitals, rotation, counts, neighbors, *refs):
    outs, (held, weights, limits, beside, sems) = refs[:-5], refs[-5:]
    copies = [
        pltpu.make_async_copy(source, target, sems.at[i])
        for i, (source, target) in enumerate(
            [(rotation, weights), (counts, limits), (orbitals, held), (neighbors, beside)]
        )
    ]
    for copy in copies:
        copy.start()
    for copy in copies[:3]:
        copy.wait()
    if shards == 2:
        near, half = outs
        rotate_kernel(shards, reach, 1, reach, held, weights, limits, half)
        rotate_kernel(shards, reach, 1, 0, held, weights, limits, near)
    else:
        for k, out in enumerate(outs):
            rotate_kernel(shards, reach, k + 1, 0, held, weights, limits, out)
    copies[3].wait()


def table_kernel(total, shards, reach, beside, limits, table):
    couplings, elems = beside.shape
    flip, groups = flipped(shards), elems // reach
    column = lax.broadcasted_iota(jnp.int32, beside.shape, 1)
    offset = beside[...] - (column + lax.axis_index("elem") * elems)
    offset = jnp.where(offset > reach, offset - total, jnp.where(offset < -reach, offset + total, offset))
    place = offset + (column - sum(jnp.where(column >= g * reach, reach, 0) for g in range(1, groups))) + reach
    past = sum(jnp.where(place >= g * reach, reach, 0) for g in range(1, groups))
    place = choose(flip, place + (elems - reach) - 2 * past, place)
    ends = limits[...].reshape(1, elems)

    def mirrored(x):
        parts = [x[:, g * reach : (g + 1) * reach] for g in reversed(range(groups))]
        return choose(flip, jnp.concatenate(parts, axis=1), x)

    rows = jnp.concatenate([mirrored(place), mirrored(ends)], axis=0)
    for e in range(elems):
        for k in range(couplings + 1):
            table[e, k] = jnp.full(table.shape[2:], rows[k, e], jnp.int32)


def pack_kernel(shards, group, blocks, packed):
    elems, couplings, _, _ = blocks.shape
    width = packed.shape[0]
    first = choose(flipped(shards), elems - (group + 1) * width, group * width)
    for e in range(width):
        for k in range(couplings):
            packed[e, :, k * FULL : (k + 1) * FULL] = blocks[first + e, k, :, :FULL]
        tail = [blocks[first + e, k, :, FULL:] for k in range(couplings)]
        packed[e, :, couplings * FULL :] = jnp.concatenate(tail, axis=1)


def middle_kernel(half, arrived, leaving, middle, copied):
    flip, share = flipped(2), half.shape[0]
    copied[...] = leaving[...]
    middle[pl.ds(choose(flip, share, 0), share)] = half[...]
    middle[pl.ds(choose(flip, 0, share), share)] = arrived[...]


def gather_kernel(shards, *refs):
    me = lax.axis_index("state")
    parts, groups, whole = refs[:shards], refs[shards : shards + 3], refs[-1]
    elems, width = parts[0].shape[0], groups[0].shape[0]
    for k, part in enumerate(parts):
        whole[pl.ds(lax.rem(me + shards - k, shards) * elems, elems)] = part[...]
    for g, group in enumerate(groups):
        group[...] = whole[g * width : (g + 1) * width]


def hard():
    return lax.rem(lax.axis_index("elem") + lax.axis_index("state"), 2)


def level_if_kernel(which, instead, body, at, *refs):
    if instead:
        other, refs = refs[at], refs[:at] + refs[at + 1 :]

        @pl.when(hard() != which)
        def _():
            refs[-2][...] = other[...]

    pl.when(hard() == which)(functools.partial(body, *refs))


def level_kernel(first, factor, with_prev, packed, table, before, here, after, *refs):
    refs, window = list(refs[:-1]), refs[-1]
    previous = refs.pop(0) if with_prev else None
    out = refs[0]
    width, rows, lanes = here.shape
    for g, group in enumerate((before, here, after)):
        window[g * width : (g + 1) * width] = group[...]
    couplings = table.shape[1] - 1
    numbers = [[table[first + e, k, 0, 0] for k in range(couplings + 1)] for e in range(width)]
    for e in range(width):
        *at, end = numbers[e]
        fields = jnp.concatenate([window[i, :FULL] for i in at] + [window[i, FULL:] for i in at], axis=0)
        image = jnp.zeros((rows, lanes), jnp.float32)
        for k in range(0, fields.shape[0], DEPTH):
            part = packed[e, :, k : k + DEPTH]
            image += jnp.dot(part, fields[k : k + DEPTH], preferred_element_type=jnp.float32)
        image = jnp.where(rows_below(end, rows, lanes), image, 0.0)
        value = factor * (image - center_shift * here[e].astype(jnp.float32)) / half_span
        if with_prev:
            value = value - previous[e].astype(jnp.float32)
        out[e] = value.astype(jnp.bfloat16)
    if len(refs) > 1:
        share = refs[1].shape[0]
        refs[1][...] = out[pl.ds(choose(flipped(2), 0, width - share), share)]


def scatter_kernel(shards, *refs):
    me = lax.axis_index("state")
    groups, parts, whole = refs[:3], refs[3:-1], refs[-1]
    elems, width = parts[0].shape[0], groups[0].shape[0]
    for g, group in enumerate(groups):
        whole[g * width : (g + 1) * width] = group[...]
    for k, part in enumerate(parts):
        part[...] = whole[pl.ds(lax.rem(me + k, shards) * elems, elems)]


def place(shards, k, first, part, out, sem):
    elems, _, lanes = part.shape
    at = lax.rem(lax.axis_index("state") + shards - k, shards) * lanes
    return pltpu.make_async_copy(part, out.at[pl.ds(first, elems), :, pl.ds(pl.multiple_of(at, lanes), lanes)], sem)


def run(copies):
    for copy in copies:
        copy.start()
    for copy in copies:
        copy.wait()


def near_copy(k, near, out, sem):
    return place(2, k, choose(flipped(2), out.shape[0] - near.shape[0], 0), near, out, sem)


def half_copy(k, half, out, sem):
    return place(2, k, choose(flipped(2), 0, out.shape[0] - half.shape[0]), half, out, sem)


def own_kernel(near, middle, half, out, sems):
    share = half.shape[0]
    kept = middle.at[pl.ds(choose(flipped(2), share, 0), share)]
    run([near_copy(0, near, out, sems.at[0]), half_copy(0, kept, out, sems.at[1]), half_copy(1, half, out, sems.at[2])])


def others_kernel(far, out, sem):
    run([near_copy(1, far, out, sem)])


def join_kernel(shards, *refs):
    parts, out, sems = refs[:shards], refs[-2], refs[-1]
    run([place(shards, k, 0, part, out, sems.at[k]) for k, part in enumerate(parts)])


def on_device(orbitals, rotation, counts, neighbors, blocks):
    row_elems, rows, states = orbitals.shape
    elems, couplings = neighbors.shape
    inputs = [
        pltpu.with_memory_space_constraint(x, pltpu.HBM) for x in (orbitals, rotation, counts, neighbors.T)
    ]
    shards = lax.axis_size("state")
    ring = lax.axis_size("elem")
    width = elems // 3
    lanes = states // shards
    group, part = bf16(width, rows, lanes), bf16(row_elems, rows, lanes)
    half = bf16(row_elems - width, rows, lanes)
    whole = pltpu.VMEM((elems, rows, lanes), jnp.bfloat16)
    dma = pltpu.SemaphoreType.DMA
    pair = shards == 2

    def permuted(x, target):
        moves = []
        for i in range(ring):
            for j in range(shards):
                to_i, to_j = target(i, j)
                moves.append((i * shards + j, to_i % ring * shards + to_j))
        return lax.ppermute(x, ("elem", "state"), moves)

    def shifted(x, step, across=False):
        return permuted(x, lambda i, j: (i + (-step if pair and j == 1 else step), 1 - j if across else j))

    def to_far_of_neighbor(x):
        return shifted(x, -1)

    def to_near_of_neighbor(x):
        return shifted(x, 1)

    def swapped(parts):
        return [
            lax.ppermute(x, "state", [(i, (i + k + 1) % shards) for i in range(shards)]) for k, x in enumerate(parts)
        ]

    *parts, held, weights, limits, beside = call(
        functools.partial(fetch_kernel, shards, width),
        ([group, half] if pair else [part] * (shards - 1)) + [jax.ShapeDtypeStruct(x.shape, x.dtype) for x in inputs],
        [HBM] * len(inputs),
        *inputs,
        scratch=[dma((4,))],
        flops=LONG,
        name="fetch",
    )
    if pair:
        leaving = parts[0]
        arrived_half = swapped(parts[1:])[0]
        near_halo = shifted(leaving, -1, across=True)
        kept = call(
            functools.partial(without, functools.partial(rotate_kernel, shards, width, 0, 0), 3, 1),
            [group, half],
            [VMEM] * 3 + [ANY],
            held,
            weights,
            limits,
            leaving,
            name="rotate_in",
        )
        far_halo = to_far_of_neighbor(kept[0])
    else:
        arrived = swapped(parts)
        kept = call(
            functools.partial(rotate_kernel, shards, width, 0, 0), [part], [VMEM] * 3, held, weights, limits, name="rotate_in"
        )
    table = call(
        functools.partial(without, functools.partial(table_kernel, elems * ring, shards, width), 2, 1),
        [jax.ShapeDtypeStruct((elems, couplings + 1, 8, 128), jnp.int32)],
        [VMEM, VMEM, ANY],
        beside,
        limits,
        kept[0],
        name="table",
    )[0]

    def pack(g, behind):
        return call(
            functools.partial(without, functools.partial(pack_kernel, shards, g), 1, 1),
            [bf16(width, rows, couplings * rows)],
            [VMEM, ANY],
            blocks,
            behind,
            name="pack",
        )[0]

    packed = {0: pack(0, table)}
    packed[2] = pack(2, packed[0])
    packed[1] = pack(1, packed[2])
    if pair:
        near = kept[0]
        middle, leaving = call(
            functools.partial(without, middle_kernel, 3, 1),
            [group] * 2,
            [VMEM] * 3 + [ANY],
            kept[1],
            arrived_half,
            leaving,
            packed[1],
            flops=SHORT,
            name="gather",
        )
        far = swapped([leaving])[0]
    else:
        near, middle, far = call(
            functools.partial(without, functools.partial(gather_kernel, shards), shards, 1),
            [group] * 3,
            [VMEM] * shards + [ANY],
            *kept,
            *arrived,
            packed[1],
            scratch=[whole],
            name="gather",
        )
        near_halo, far_halo = to_near_of_neighbor(far), to_far_of_neighbor(near)

    def level(g, m, before, here, after, previous, which=None, instead=None, split=False, behind=(), flops=0):
        body = functools.partial(level_kernel, g * width, 1.0 if m == 1 else 2.0, previous is not None)
        args = [packed[g], table, before, here, after] + ([] if previous is None else [previous])
        if which is not None:
            body = functools.partial(level_if_kernel, which, instead is not None, body, len(args))
            args += [] if instead is None else [instead]
        specs = [VMEM] * len(args)
        if behind:
            body = functools.partial(without, body, len(args), len(behind))
            args, specs = args + list(behind), specs + [ANY] * len(behind)
        outs = call(
            body,
            [group] + [half] * split,
            specs,
            *args,
            scratch=[pltpu.VMEM((3 * width, rows, lanes), jnp.bfloat16)],
            flops=flops,
            name=("near", "middle", "far")[g] + str(m),
        )
        return outs if split else outs[0]

    older = (None, None, None)
    for m in range(1, DEG + 1):
        last = m == DEG
        if m == 1:
            new_near = level(0, m, near_halo, near, middle, older[0])
            next_far_halo = to_far_of_neighbor(new_near)
            new_far = level(2, m, middle, far, far_halo, older[2], behind=[new_near])
            next_near_halo = to_near_of_neighbor(new_far)
            new_middle = level(1, m, near, middle, far, older[1])
        elif m % 2:
            new_middle = level(1, m, near, middle, far, older[1])
            new_near = level(0, m, near_halo, near, middle, older[0], behind=[new_middle])
            next_far_halo = to_far_of_neighbor(new_near)
            new_far = level(2, m, middle, far, far_halo, older[2], behind=[new_near])
            next_near_halo = to_near_of_neighbor(new_far)
        elif not last:
            new_far = level(2, m, middle, far, far_halo, older[2])
            next_near_halo = to_near_of_neighbor(new_far)
            new_middle = level(1, m, near, middle, far, older[1], behind=[new_far])
            new_near = level(0, m, near_halo, near, middle, older[0], behind=[new_middle])
            next_far_halo = to_far_of_neighbor(new_near)
        else:
            if pair:
                mate_halo = permuted(near, lambda i, j: (i ^ 1, j))
                early = level(2, m, middle, far, mate_halo, older[2], which=0)
                new_middle, half_leaving = level(1, m, near, middle, far, older[1], split=True, behind=[early])
                half_arrived = swapped([half_leaving])[0]
                new_far = level(2, m, middle, far, far_halo, older[2], which=1, instead=early)
                arrived = swapped([new_far])[0]
            else:
                new_middle = level(1, m, near, middle, far, older[1])
                new_far = level(2, m, middle, far, far_halo, older[2])
            behind = [half_arrived] if pair else []
            new_near = level(0, m, near_halo, near, middle, older[0], behind=behind, flops=LONG)
        if not last:
            near_halo, far_halo = next_near_halo, next_far_halo
        older, (near, middle, far) = (near, middle, far), (new_near, new_middle, new_far)

    whole_out = [bf16(*orbitals.shape)]
    if pair:
        out = call(
            own_kernel,
            whole_out,
            [VMEM] * 3,
            near,
            middle,
            half_arrived,
            out_specs=[HBM],
            scratch=[dma((3,))],
            name="own",
        )[0]
        return call(
            functools.partial(without, others_kernel, 1, 1),
            whole_out,
            [VMEM, HBM],
            arrived,
            out,
            out_specs=[HBM],
            scratch=[dma],
            aliases={1: 0},
            name="others",
        )[0]
    kept, *parts = call(
        functools.partial(scatter_kernel, shards),
        [part] * shards,
        [VMEM] * 3,
        near,
        middle,
        far,
        scratch=[whole],
        name="scatter",
    )
    return call(
        functools.partial(join_kernel, shards),
        whole_out,
        [VMEM] * shards,
        kept,
        *swapped(parts),
        out_specs=[HBM],
        scratch=[dma((shards,))],
        name="join",
    )[0]


def solution(mesh):
    in_specs = (
        P(("elem", "state"), None, None),
        P(),
        P("elem"),
        P("elem", None),
        P("elem", None, None, None),
    )
    out_specs = P(("elem", "state"), None, None)
    return jax.shard_map(on_device, mesh=mesh, in_specs=in_specs, out_specs=out_specs, check_vma=False)
```

```python
import functools

import jax
import jax.numpy as jnp
from jax import lax
from jax.experimental import pallas as pl
from jax.experimental.pallas import tpu as pltpu
from jax.sharding import PartitionSpec as P

DEG = 4
FULL = 128
DEPTH = 768
LONG, SHORT = 20 * 10**9, 10**9

center_shift = 0.2
half_span = 1.1

VMEM = pl.BlockSpec(memory_space=pltpu.VMEM)
HBM = pl.BlockSpec(memory_space=pltpu.HBM)
ANY = pl.BlockSpec(memory_space=pl.ANY)


def call(kernel, outs, ins, *args, out_specs=None, scratch=(), aliases=None, limit=4 << 20, flops=0, name=None):
    return pl.pallas_call(
        kernel,
        out_shape=outs,
        in_specs=ins,
        out_specs=out_specs or [VMEM] * len(outs),
        scratch_shapes=list(scratch),
        input_output_aliases=aliases or {},
        compiler_params=pltpu.CompilerParams(vmem_limit_bytes=limit),
        cost_estimate=pl.CostEstimate(flops=flops, bytes_accessed=1024, transcendentals=0),
        name=name,
    )(*args)


def bf16(*shape):
    return jax.ShapeDtypeStruct(shape, jnp.bfloat16)


def without(body, at, count, *refs):
    body(*refs[:at], *refs[at + count :])


def flipped(shards):
    return lax.axis_index("state") == 1 if shards == 2 else False


def choose(flip, yes, no):
    return no if flip is False else jnp.where(flip, yes, no)


def rows_below(count, rows, lanes):
    return lax.broadcasted_iota(jnp.int32, (rows, lanes), 0) < count


def turn(shards, k, element, weights, count):
    rows, lanes = element.shape[0], weights.shape[1] // shards
    at = lax.rem(lax.axis_index("state") + k, shards) * lanes
    turned = jnp.dot(element, weights[:, pl.ds(pl.multiple_of(at, lanes), lanes)], preferred_element_type=jnp.float32)
    return jnp.where(rows_below(count, rows, lanes), turned, 0.0).astype(jnp.bfloat16)


def rotate_kernel(shards, reach, k, first, held, weights, limits, *outs):
    me, flip = lax.axis_index("state"), flipped(shards)
    elems = held.shape[0]
    ends = limits[...]
    spots = [(out, e) for out in outs for e in range(out.shape[0])]
    for spot, (out, at) in enumerate(spots, first):
        e = choose(flip, (spot + elems - reach) % elems, spot)
        count = ends[spot]
        for shard in range(shards):
            here = (spot + elems - reach) % elems if shard == 1 and flip is not False else spot
            count = jnp.where(me == shard, ends[shard * elems + here], count)
        out[at] = turn(shards, k, held[e], weights, count)


def fetch_kernel(shards, reach, orbitals, rotation, counts, neighbors, *refs):
    outs, (held, weights, limits, beside, sems) = refs[:-5], refs[-5:]
    copies = [
        pltpu.make_async_copy(source, target, sems.at[i])
        for i, (source, target) in enumerate(
            [(rotation, weights), (counts, limits), (orbitals, held), (neighbors, beside)]
        )
    ]
    for copy in copies:
        copy.start()
    for copy in copies[:3]:
        copy.wait()
    if shards == 2:
        near, half = outs
        rotate_kernel(shards, reach, 1, reach, held, weights, limits, half)
        rotate_kernel(shards, reach, 1, 0, held, weights, limits, near)
    else:
        for k, out in enumerate(outs):
            rotate_kernel(shards, reach, k + 1, 0, held, weights, limits, out)
    copies[3].wait()


def table_kernel(total, shards, reach, beside, limits, table):
    couplings, elems = beside.shape
    flip, groups = flipped(shards), elems // reach
    column = lax.broadcasted_iota(jnp.int32, beside.shape, 1)
    offset = beside[...] - (column + lax.axis_index("elem") * elems)
    offset = jnp.where(offset > reach, offset - total, jnp.where(offset < -reach, offset + total, offset))
    place = offset + (column - sum(jnp.where(column >= g * reach, reach, 0) for g in range(1, groups))) + reach
    past = sum(jnp.where(place >= g * reach, reach, 0) for g in range(1, groups))
    place = choose(flip, place + (elems - reach) - 2 * past, place)
    ends = limits[...].reshape(1, elems)

    def mirrored(x):
        parts = [x[:, g * reach : (g + 1) * reach] for g in reversed(range(groups))]
        return choose(flip, jnp.concatenate(parts, axis=1), x)

    rows = jnp.concatenate([mirrored(place), mirrored(ends)], axis=0)
    for e in range(elems):
        for k in range(couplings + 1):
            table[e, k] = jnp.full(table.shape[2:], rows[k, e], jnp.int32)


def pack_kernel(shards, group, blocks, packed):
    elems, couplings, _, _ = blocks.shape
    width = packed.shape[0]
    first = choose(flipped(shards), elems - (group + 1) * width, group * width)
    for e in range(width):
        for k in range(couplings):
            packed[e, :, k * FULL : (k + 1) * FULL] = blocks[first + e, k, :, :FULL]
        tail = [blocks[first + e, k, :, FULL:] for k in range(couplings)]
        packed[e, :, couplings * FULL :] = jnp.concatenate(tail, axis=1)


def middle_kernel(half, arrived, leaving, middle, copied):
    flip, share = flipped(2), half.shape[0]
    copied[...] = leaving[...]
    middle[pl.ds(choose(flip, share, 0), share)] = half[...]
    middle[pl.ds(choose(flip, 0, share), share)] = arrived[...]


def gather_kernel(shards, *refs):
    me = lax.axis_index("state")
    parts, groups, whole = refs[:shards], refs[shards : shards + 3], refs[-1]
    elems, width = parts[0].shape[0], groups[0].shape[0]
    for k, part in enumerate(parts):
        whole[pl.ds(lax.rem(me + shards - k, shards) * elems, elems)] = part[...]
    for g, group in enumerate(groups):
        group[...] = whole[g * width : (g + 1) * width]


def hard():
    return lax.rem(lax.axis_index("elem") + lax.axis_index("state"), 2)


def level_if_kernel(which, instead, body, at, *refs):
    if instead:
        other, refs = refs[at], refs[:at] + refs[at + 1 :]

        @pl.when(hard() != which)
        def _():
            refs[-2][...] = other[...]

    pl.when(hard() == which)(functools.partial(body, *refs))


def level_kernel(first, factor, with_prev, packed, table, before, here, after, *refs):
    refs, window = list(refs[:-1]), refs[-1]
    previous = refs.pop(0) if with_prev else None
    out = refs[0]
    width, rows, lanes = here.shape
    for g, group in enumerate((before, here, after)):
        window[g * width : (g + 1) * width] = group[...]
    couplings = table.shape[1] - 1
    numbers = [[table[first + e, k, 0, 0] for k in range(couplings + 1)] for e in range(width)]
    for e in range(width):
        *at, end = numbers[e]
        fields = jnp.concatenate([window[i, :FULL] for i in at] + [window[i, FULL:] for i in at], axis=0)
        image = jnp.zeros((rows, lanes), jnp.float32)
        for k in range(0, fields.shape[0], DEPTH):
            part = packed[e, :, k : k + DEPTH]
            image += jnp.dot(part, fields[k : k + DEPTH], preferred_element_type=jnp.float32)
        image = jnp.where(rows_below(end, rows, lanes), image, 0.0)
        value = factor * (image - center_shift * here[e].astype(jnp.float32)) / half_span
        if with_prev:
            value = value - previous[e].astype(jnp.float32)
        out[e] = value.astype(jnp.bfloat16)
    if len(refs) > 1:
        share = refs[1].shape[0]
        refs[1][...] = out[pl.ds(choose(flipped(2), 0, width - share), share)]


def scatter_kernel(shards, *refs):
    me = lax.axis_index("state")
    groups, parts, whole = refs[:3], refs[3:-1], refs[-1]
    elems, width = parts[0].shape[0], groups[0].shape[0]
    for g, group in enumerate(groups):
        whole[g * width : (g + 1) * width] = group[...]
    for k, part in enumerate(parts):
        part[...] = whole[pl.ds(lax.rem(me + k, shards) * elems, elems)]


def place(shards, k, first, part, out, sem):
    elems, _, lanes = part.shape
    at = lax.rem(lax.axis_index("state") + shards - k, shards) * lanes
    return pltpu.make_async_copy(part, out.at[pl.ds(first, elems), :, pl.ds(pl.multiple_of(at, lanes), lanes)], sem)


def run(copies):
    for copy in copies:
        copy.start()
    for copy in copies:
        copy.wait()


def near_copy(k, near, out, sem):
    return place(2, k, choose(flipped(2), out.shape[0] - near.shape[0], 0), near, out, sem)


def half_copy(k, half, out, sem):
    return place(2, k, choose(flipped(2), 0, out.shape[0] - half.shape[0]), half, out, sem)


def own_kernel(near, middle, half, out, sems):
    share = half.shape[0]
    kept = middle.at[pl.ds(choose(flipped(2), share, 0), share)]
    run([near_copy(0, near, out, sems.at[0]), half_copy(0, kept, out, sems.at[1]), half_copy(1, half, out, sems.at[2])])


def others_kernel(far, out, sem):
    run([near_copy(1, far, out, sem)])


def join_kernel(shards, *refs):
    parts, out, sems = refs[:shards], refs[-2], refs[-1]
    run([place(shards, k, 0, part, out, sems.at[k]) for k, part in enumerate(parts)])


def on_device(orbitals, rotation, counts, neighbors, blocks):
    row_elems, rows, states = orbitals.shape
    elems, couplings = neighbors.shape
    inputs = [
        pltpu.with_memory_space_constraint(x, pltpu.HBM) for x in (orbitals, rotation, counts, neighbors.T)
    ]
    shards = lax.axis_size("state")
    ring = lax.axis_size("elem")
    width = elems // 3
    lanes = states // shards
    group, part = bf16(width, rows, lanes), bf16(row_elems, rows, lanes)
    half = bf16(row_elems - width, rows, lanes)
    whole = pltpu.VMEM((elems, rows, lanes), jnp.bfloat16)
    dma = pltpu.SemaphoreType.DMA
    pair = shards == 2

    def permuted(x, target):
        moves = []
        for i in range(ring):
            for j in range(shards):
                to_i, to_j = target(i, j)
                moves.append((i * shards + j, to_i % ring * shards + to_j))
        return lax.ppermute(x, ("elem", "state"), moves)

    def shifted(x, step, across=False):
        return permuted(x, lambda i, j: (i + (-step if pair and j == 1 else step), 1 - j if across else j))

    def to_far_of_neighbor(x):
        return shifted(x, -1)

    def to_near_of_neighbor(x):
        return shifted(x, 1)

    def swapped(parts):
        return [
            lax.ppermute(x, "state", [(i, (i + k + 1) % shards) for i in range(shards)]) for k, x in enumerate(parts)
        ]

    *parts, held, weights, limits, beside = call(
        functools.partial(fetch_kernel, shards, width),
        ([group, half] if pair else [part] * (shards - 1)) + [jax.ShapeDtypeStruct(x.shape, x.dtype) for x in inputs],
        [HBM] * len(inputs),
        *inputs,
        scratch=[dma((4,))],
        flops=LONG,
        name="fetch",
    )
    if pair:
        leaving = parts[0]
        arrived_half = swapped(parts[1:])[0]
        near_halo = shifted(leaving, -1, across=True)
        kept = call(
            functools.partial(without, functools.partial(rotate_kernel, shards, width, 0, 0), 3, 1),
            [group, half],
            [VMEM] * 3 + [ANY],
            held,
            weights,
            limits,
            leaving,
            name="rotate_in",
        )
        far_halo = to_far_of_neighbor(kept[0])
    else:
        arrived = swapped(parts)
        kept = call(
            functools.partial(rotate_kernel, shards, width, 0, 0), [part], [VMEM] * 3, held, weights, limits, name="rotate_in"
        )
    table = call(
        functools.partial(without, functools.partial(table_kernel, elems * ring, shards, width), 2, 1),
        [jax.ShapeDtypeStruct((elems, couplings + 1, 8, 128), jnp.int32)],
        [VMEM, VMEM, ANY],
        beside,
        limits,
        kept[0],
        name="table",
    )[0]

    def pack(g, behind):
        return call(
            functools.partial(without, functools.partial(pack_kernel, shards, g), 1, 1),
            [bf16(width, rows, couplings * rows)],
            [VMEM, ANY],
            blocks,
            behind,
            name="pack",
        )[0]

    packed = {0: pack(0, table)}
    packed[2] = pack(2, packed[0])
    packed[1] = pack(1, packed[2])
    if pair:
        near = kept[0]
        middle, leaving = call(
            functools.partial(without, middle_kernel, 3, 1),
            [group] * 2,
            [VMEM] * 3 + [ANY],
            kept[1],
            arrived_half,
            leaving,
            packed[1],
            flops=SHORT,
            name="gather",
        )
        far = swapped([leaving])[0]
    else:
        near, middle, far = call(
            functools.partial(without, functools.partial(gather_kernel, shards), shards, 1),
            [group] * 3,
            [VMEM] * shards + [ANY],
            *kept,
            *arrived,
            packed[1],
            scratch=[whole],
            name="gather",
        )
        near_halo, far_halo = to_near_of_neighbor(far), to_far_of_neighbor(near)

    def level(g, m, before, here, after, previous, which=None, instead=None, split=False, behind=(), flops=0):
        body = functools.partial(level_kernel, g * width, 1.0 if m == 1 else 2.0, previous is not None)
        args = [packed[g], table, before, here, after] + ([] if previous is None else [previous])
        if which is not None:
            body = functools.partial(level_if_kernel, which, instead is not None, body, len(args))
            args += [] if instead is None else [instead]
        specs = [VMEM] * len(args)
        if behind:
            body = functools.partial(without, body, len(args), len(behind))
            args, specs = args + list(behind), specs + [ANY] * len(behind)
        outs = call(
            body,
            [group] + [half] * split,
            specs,
            *args,
            scratch=[pltpu.VMEM((3 * width, rows, lanes), jnp.bfloat16)],
            flops=flops,
            name=("near", "middle", "far")[g] + str(m),
        )
        return outs if split else outs[0]

    older = (None, None, None)
    for m in range(1, DEG + 1):
        last = m == DEG
        if m == 1:
            new_near = level(0, m, near_halo, near, middle, older[0])
            next_far_halo = to_far_of_neighbor(new_near)
            new_far = level(2, m, middle, far, far_halo, older[2], behind=[new_near])
            next_near_halo = to_near_of_neighbor(new_far)
            new_middle = level(1, m, near, middle, far, older[1])
        elif m % 2:
            new_middle = level(1, m, near, middle, far, older[1])
            new_near = level(0, m, near_halo, near, middle, older[0], behind=[new_middle])
            next_far_halo = to_far_of_neighbor(new_near)
            new_far = level(2, m, middle, far, far_halo, older[2], behind=[new_near])
            next_near_halo = to_near_of_neighbor(new_far)
        elif not last:
            new_far = level(2, m, middle, far, far_halo, older[2])
            next_near_halo = to_near_of_neighbor(new_far)
            new_middle = level(1, m, near, middle, far, older[1], behind=[new_far])
            new_near = level(0, m, near_halo, near, middle, older[0], behind=[new_middle])
            next_far_halo = to_far_of_neighbor(new_near)
        else:
            if pair:
                mate_halo = permuted(near, lambda i, j: (i ^ 1, j))
                early = level(2, m, middle, far, mate_halo, older[2], which=0)
                new_middle, half_leaving = level(1, m, near, middle, far, older[1], split=True, behind=[early])
                half_arrived = swapped([half_leaving])[0]
                new_far = level(2, m, middle, far, far_halo, older[2], which=1, instead=early)
                arrived = swapped([new_far])[0]
            else:
                new_middle = level(1, m, near, middle, far, older[1])
                new_far = level(2, m, middle, far, far_halo, older[2])
            behind = [half_arrived] if pair else []
            new_near = level(0, m, near_halo, near, middle, older[0], behind=behind, flops=LONG)
        if not last:
            near_halo, far_halo = next_near_halo, next_far_halo
        older, (near, middle, far) = (near, middle, far), (new_near, new_middle, new_far)

    whole_out = [bf16(*orbitals.shape)]
    if pair:
        out = call(
            own_kernel,
            whole_out,
            [VMEM] * 3,
            near,
            middle,
            half_arrived,
            out_specs=[HBM],
            scratch=[dma((3,))],
            name="own",
        )[0]
        return call(
            functools.partial(without, others_kernel, 1, 1),
            whole_out,
            [VMEM, HBM],
            arrived,
            out,
            out_specs=[HBM],
            scratch=[dma],
            aliases={1: 0},
            name="others",
        )[0]
    kept, *parts = call(
        functools.partial(scatter_kernel, shards),
        [part] * shards,
        [VMEM] * 3,
        near,
        middle,
        far,
        scratch=[whole],
        name="scatter",
    )
    return call(
        functools.partial(join_kernel, shards),
        whole_out,
        [VMEM] * shards,
        kept,
        *swapped(parts),
        out_specs=[HBM],
        scratch=[dma((shards,))],
        name="join",
    )[0]


def solution(mesh):
    in_specs = (
        P(("elem", "state"), None, None),
        P(),
        P("elem"),
        P("elem", None),
        P("elem", None, None, None),
    )
    out_specs = P(("elem", "state"), None, None)
    return jax.shard_map(on_device, mesh=mesh, in_specs=in_specs, out_specs=out_specs, check_vma=False)
```
